256 devices in a mesh: pole: 4 (over y), blk: 64 (over x, z, core).
Axes of the slice: x: 4, y: 4, z: 8, core: 2. Of those that a mesh axis runs over, the one named last changes fastest.
Arguments:
- inverse_blocks: bfloat16 [8, 65536, 2048], P('pole', 'blk'), may hold values from -6 to 6
- panel_blocks: bfloat16 [8, 8192, 1024], P('pole', 'blk'), may hold values from -0.046875 to 0.046875
- ancestor_mask: int32 [64, 4], P('blk'), may hold values 0 or 1
- diag_inverse: float32 [8, 512, 256], P('pole', 'blk'), may hold values from -6 to 6
- pole_weights: float32 [8, 2], replicated, may hold values from -6 to 6
- pole_order: int32 [8], replicated, may hold values from 0 to 7, each once
Outputs:
- density_columns: float32 [8192, 512], P('blk', 'pole')
- density_diag: float32 [512, 128], P('blk', 'pole')
The draws below stay inside these ranges and needn't reach their ends.
Inputs may be any that keep to these rules, and one draw needn't show every extreme that they name: `pole_order`: each data position names a different pole number.
All inputs are finite; a program needn't handle non-finite values. No bound on the sum of `ancestor_mask` on one device may be relied on, other than what follows from the above.
Results may differ from the reference program's by a relative error of at most 0.0003.
Values may be sent and summed in bfloat16 or wider, within the bound.
No kernel may reach another device: no remote copies, remote signals or barrier semaphores. Data moves between devices by JAX's collectives and lax.ppermute only.
A program may use at most 128 MiB of HBM per device.

```python
import jax
import jax.numpy as jnp
from jax import lax

W = 128
S = 4
PC = 8
POLES = 8
NA = 64
PR = 8
N_BLK = 64


def plant(values, key, low, high):
    shape = values.shape
    index_at = [jax.random.randint(jax.random.fold_in(key, axis), (), 0, shape[axis]) for axis in range(len(shape))]
    values = values.at[tuple(index_at)].set(low)
    longest = shape.index(max(shape))
    index_at[longest] = (index_at[longest] + 1) % shape[longest]
    return values.at[tuple(index_at)].set(high)


def level_of(stream_key, dims, pieces, low, largest):
    def one(axis_at, blocks):
        draws = jax.random.uniform(jax.random.fold_in(jax.random.fold_in(stream_key, 6), axis_at), (blocks,), jnp.float32, low / len(pieces), largest / len(pieces))
        return jnp.repeat(jnp.exp(draws), dims[axis_at] // blocks).reshape((-1,) + (1,) * (len(dims) - axis_at - 1))

    loudness = one(*pieces[0])
    for cut in pieces[1:]:
        loudness = loudness * one(*cut)
    return loudness


def bell_draw(stream_key, shape, width, reach, pieces=(), kind=jnp.bfloat16):
    level = level_of(stream_key, shape, pieces, -0.22, 0.18) if pieces else 1.0
    values = jax.random.normal(stream_key, shape, jnp.float32) * width * level
    return jnp.minimum(jnp.maximum(values, -reach), reach).astype(kind)


def setup_inputs(seed: int = 0) -> dict:
    keys = jax.random.split(jax.random.key(seed), 7)
    inverse_blocks = bell_draw(keys[0], (POLES, N_BLK * PC * W, PR * 2 * W), 1.0, 6.0, ((0, 4), (1, 64)))
    panel_blocks = bell_draw(keys[1], (POLES, NA * W, 2 * S * W), (2 * W * NA) ** -0.5, 0.046875, ((0, 4), (1, 64)))
    ancestor_mask = plant((jax.random.randint(keys[2], (NA, S), 0, 4) < 3).astype(jnp.int32), jax.random.fold_in(keys[2], 1), 0, 1)
    diag_inverse = bell_draw(keys[3], (POLES, S * W, 2 * W), 1.0, 6.0, ((0, 4), (1, 64)), jnp.float32)
    pole_weights = bell_draw(keys[4], (POLES, 2), 1.0, 6.0, (), jnp.float32)
    pole_order = jax.random.permutation(keys[5], POLES).astype(jnp.int32)
    return dict(inverse_blocks=inverse_blocks, panel_blocks=panel_blocks, ancestor_mask=ancestor_mask, diag_inverse=diag_inverse, pole_weights=pole_weights, pole_order=pole_order)


def trace_parts(left_real, left_imag, right_real, right_imag):
    form = "iukx,iuky->kxy"
    high = lax.Precision.HIGHEST
    real_part = jnp.einsum(form, left_real, right_real, precision=high) - jnp.einsum(form, left_imag, right_imag, precision=high)
    imag_part = jnp.einsum(form, left_real, right_imag, precision=high) + jnp.einsum(form, left_imag, right_real, precision=high)
    return real_part, imag_part


def reference(inverse_blocks, panel_blocks, ancestor_mask, diag_inverse, pole_weights, pole_order):
    span = S * W
    mask_bf = ancestor_mask.astype(jnp.bfloat16)[:, None, None, :, None]
    mask_f = ancestor_mask.astype(jnp.float32)
    density_sum = jnp.zeros((NA, W, S, W), jnp.float32)
    diag_sum = jnp.zeros((S, W, W), jnp.float32)
    for position in range(POLES):
        pole_id = pole_order[position]
        weight_real = pole_weights[pole_id, 0]
        weight_imag = pole_weights[pole_id, 1]
        masked = (panel_blocks[position].reshape(NA, W, 2, S, W) * mask_bf).reshape(NA, W, 2 * span)
        blocks = masked.reshape(PR, PC, W, 2 * span)
        lower_rows = jnp.concatenate([-blocks[..., span:], blocks[..., :span]], axis=-1)
        real_form = jnp.concatenate([blocks, lower_rows], axis=2)
        inverse_mat = inverse_blocks[position].reshape(PR, PC, PC * W, PR, 2 * W)
        selected = -jnp.einsum("rbmas,absn->rmn", inverse_mat.astype(jnp.float32), real_form.astype(jnp.float32))
        selected = selected.reshape(NA, W, 2, S, W)
        sel_real = selected[:, :, 0]
        sel_imag = selected[:, :, 1]
        density_sum = density_sum + weight_real * sel_real - weight_imag * sel_imag
        panel_f = masked.astype(jnp.float32).reshape(NA, W, 2, S, W)
        term_real, term_imag = trace_parts(panel_f[:, :, 0], panel_f[:, :, 1], sel_real, sel_imag)
        diag_blocks = diag_inverse[position].reshape(S, W, 2 * W)
        diag_sum = diag_sum + weight_real * (diag_blocks[..., :W] - term_real) - weight_imag * (diag_blocks[..., W:] - term_imag)
    density_sum = density_sum * mask_f[:, None, :, None]
    return density_sum.reshape(NA * W, span), diag_sum.reshape(span, W)
```

```python
import jax
import jax.numpy as jnp
from jax import lax
from jax.experimental import pallas as pl
from jax.experimental.pallas import tpu as pltpu
from jax.sharding import PartitionSpec as P

X, Z, C, Y = 4, 8, 2, 4
ROWS = 256


def place(x, z, core):
    return (x % X) * Z * C + (z % Z) * C + core


PLACES = [(x, z, core) for x in range(X) for z in range(Z) for core in range(C)]


def along_x(value, by):
    return lax.ppermute(value, "blk", [(place(*at), place(at[0] + by, at[1], at[2])) for at in PLACES])


def along_z(value, by):
    return lax.ppermute(value, "blk", [(place(*at), place(at[0], at[1] + by, at[2])) for at in PLACES])


def z_partner(value, bits):
    return lax.ppermute(value, "blk", [(place(*at), place(at[0], at[1] ^ bits, at[2])) for at in PLACES])


def other_core(value):
    return lax.ppermute(value, "blk", [(place(*at), place(at[0], at[1], 1 - at[2])) for at in PLACES])


def build_form(form_ref, panels):
    half = panels[0].shape[1] // 2
    for step, panel_ref in enumerate(panels):
        top = step * 256
        panel = panel_ref[...]
        form_ref[top : top + 128, :] = panel
        form_ref[top + 128 : top + 256, :half] = -panel[:, half:]
        form_ref[top + 128 : top + 256, half:] = panel[:, :half]


def first_kernel(meta, a0, a1, a2, a3, *rest):
    panels, out, form = rest[:8], rest[8], rest[9]
    pole, tile = pl.program_id(0), pl.program_id(1)
    for which in range(2):
        @pl.when((tile == 0) & (pole == which))
        def _():
            build_form(form, panels[4 * which : 4 * which + 4])

    left = jnp.concatenate([a[0] for a in (a0, a1, a2, a3)], axis=1)
    out[0] = jnp.dot(left, form[...], preferred_element_type=jnp.float32)


def second_kernel(meta, weights, order, a0, a1, a2, a3, before, *rest):
    panels, (keep, send, parts), form = rest[:8], rest[8:11], rest[11]
    tile, pole = pl.program_id(0), pl.program_id(1)
    for which in range(2):
        @pl.when((tile == 0) & (pole == which))
        def _():
            build_form(form.at[which], panels[4 * which : 4 * which + 4])

    left = jnp.concatenate([a[0] for a in (a0, a1, a2, a3)], axis=1)
    total = before[0] + jnp.dot(left, form[pole], preferred_element_type=jnp.float32)
    number = order[meta[5] * 2 + pole]
    w_re, w_im = weights[number, 0], weights[number, 1]
    half = total.shape[1] // 2
    real, imag = total[:, :half], total[:, half:]
    q_re = w_re * real - w_im * imag
    q_im = -(w_re * imag + w_im * real)
    core = meta[4]
    for k in range(4):
        for side, q in enumerate((q_re, q_im)):
            value = q[:, k * 128 : k * 128 + 128]
            high = value.astype(jnp.bfloat16)
            low = (value - high.astype(jnp.float32)).astype(jnp.bfloat16)
            for c in range(2):
                parts[k, c, 0, side, :, :128] = high[c * 128 : c * 128 + 128]
                parts[k, c, 0, side, :, 128:] = low[c * 128 : c * 128 + 128]
        even = q_re[:128, k * 128 : k * 128 + 128]
        odd = q_re[128:, k * 128 : k * 128 + 128]
        kept = jnp.where(core == 0, even, odd)
        sent = jnp.where(core == 0, odd, even)

        @pl.when(pole == 0)
        def _():
            keep[k, 0] = -kept
            send[k, 0] = -sent

        @pl.when(pole == 1)
        def _():
            keep[k, 0] = keep[k, 0] - kept
            send[k, 0] = send[k, 0] - sent


def flip_kernel(panel0, panel1, *outs):
    for p, panel in enumerate((panel0, panel1)):
        for part in range(8):
            outs[0][p, part] = panel[:, part * 128 : part * 128 + 128].T


def trace_kernel(meta, weights, order, parts, diag, *rest):
    pieces, (keep, send), total = rest[:10], rest[10:12], rest[12]
    k = pl.program_id(0)
    total[...] = jnp.zeros_like(total)
    core = meta[4]
    for index, piece in enumerate(pieces):
        place_c = meta[8 + index]

        @pl.when(place_c >= 0)
        def _():
            left = jnp.concatenate(
                [piece[p, side * 4 + k] for p in range(2) for side in range(2)], axis=1
            )
            right = parts[0, place_c].reshape(512, 256)
            total[...] += jnp.dot(left, right, preferred_element_type=jnp.float32)

    value = (total[:, :128] + total[:, 128:]).reshape(8, 2, 8, 128)
    keep[0] = jnp.where(core == 0, value[:, 0], value[:, 1])
    send[0] = jnp.where(core == 0, value[:, 1], value[:, 0])

    @pl.when(k == meta[6])
    def _():
        mine = jnp.zeros((8, 128), jnp.float32)
        for p in range(2):
            number = order[meta[5] * 2 + p]
            mine += weights[number, 0] * diag[p, :, :128] - weights[number, 1] * diag[p, :, 128:]
        keep[0, meta[7]] += mine


def smem():
    return pl.BlockSpec(memory_space=pltpu.SMEM)


def per_device(inverse_blocks, panel_blocks, ancestor_mask, diag_inverse, pole_weights, pole_order):
    rank = lax.axis_index("blk")
    y = lax.axis_index("pole")
    xc, z, core = rank // (Z * C), (rank // C) % Z, rank % C
    zh, zl = z // 4, z % 4

    mask_row = jnp.broadcast_to(
        ancestor_mask[0].astype(jnp.bfloat16)[None, :, None], (2, 4, 128)
    ).reshape(1, 1024)
    own = [panel_blocks[p] * mask_row for p in range(2)]
    far = [z_partner(own[p], 4) for p in range(2)]

    def spread(pair):
        columns = []
        for p in range(2):
            right, left = along_x(pair[p], 1), along_x(pair[p], -1)
            across = along_x(right, 1) if p == 0 else along_x(left, -1)
            columns += [pair[p], right, left, across]
        return columns

    near_panels = spread(own)
    far_panels = spread(far)

    xs = [xc, (xc + 3) % 4, (xc + 1) % 4, (xc + 2) % 4]

    def meta_of(side):
        return [v * 2 + side for v in xs] + [core, y, xc, z]

    def a_spec(step, order):
        def index(*args):
            meta = args[2]
            p, m = (args[0], args[1]) if order == "pm" else (args[1], args[0])
            return (p, m, meta[step])
        return pl.BlockSpec((1, ROWS, 256), index)

    whole = pl.BlockSpec((128, 1024), lambda *args: (0, 0))
    near_meta = jnp.stack(meta_of(zh)).astype(jnp.int32)
    partial = pl.pallas_call(
        first_kernel,
        grid_spec=pltpu.PrefetchScalarGridSpec(
            num_scalar_prefetch=1,
            grid=(2, 1024 // ROWS),
            in_specs=[a_spec(s, "pm") for s in range(4)] + [whole] * 8,
            out_specs=pl.BlockSpec((1, ROWS, 1024), lambda p, m, meta: (p, m, 0)),
            scratch_shapes=[pltpu.VMEM((1024, 1024), jnp.bfloat16)],
        ),
        out_shape=jax.ShapeDtypeStruct((2, 1024, 1024), jnp.float32),
        cost_estimate=pl.CostEstimate(flops=2 * 2 * 1024**3, bytes_accessed=16 * 2**20, transcendentals=0),
        compiler_params=pltpu.CompilerParams(vmem_limit_bytes=40 * 2**20),
        name="near",
    )(near_meta, *([inverse_blocks] * 4), *near_panels)

    far_meta = jnp.stack(meta_of(1 - zh)).astype(jnp.int32)
    keep, send, parts = pl.pallas_call(
        second_kernel,
        grid_spec=pltpu.PrefetchScalarGridSpec(
            num_scalar_prefetch=3,
            grid=(1024 // ROWS, 2),
            in_specs=[a_spec(s, "mp") for s in range(4)]
            + [pl.BlockSpec((1, ROWS, 1024), lambda m, p, *_: (p, m, 0))]
            + [whole] * 8,
            out_specs=[
                pl.BlockSpec((4, 1, 128, 128), lambda m, p, *_: (0, m, 0, 0)),
                pl.BlockSpec((4, 1, 128, 128), lambda m, p, *_: (0, m, 0, 0)),
                pl.BlockSpec((4, 2, 1, 2, 128, 256), lambda m, p, *_: (0, m, p, 0, 0, 0)),
            ],
            scratch_shapes=[pltpu.VMEM((2, 1024, 1024), jnp.bfloat16)],
        ),
        out_shape=[
            jax.ShapeDtypeStruct((4, 4, 128, 128), jnp.float32),
            jax.ShapeDtypeStruct((4, 4, 128, 128), jnp.float32),
            jax.ShapeDtypeStruct((4, 8, 2, 2, 128, 256), jnp.bfloat16),
        ],
        cost_estimate=pl.CostEstimate(flops=2 * 2 * 1024**3, bytes_accessed=24 * 2**20, transcendentals=0),
        compiler_params=pltpu.CompilerParams(vmem_limit_bytes=40 * 2**20),
        name="far",
    )(far_meta, pole_weights, pole_order, *([inverse_blocks] * 4), partial, *far_panels)

    def flip(pair):
        return pl.pallas_call(
            flip_kernel,
            out_shape=jax.ShapeDtypeStruct((2, 8, 128, 128), jnp.bfloat16),
            cost_estimate=pl.CostEstimate(flops=0, bytes_accessed=2**20, transcendentals=0),
            name="flip",
        )(*pair)

    own_t, far_t = flip(own), flip(far)
    from_left, from_right = along_z(own_t, 1), along_z(own_t, -1)
    from_left2 = along_z(jnp.where(zl == 3, far_t, from_left), 1)
    from_right2 = along_z(jnp.where(zl == 0, far_t, from_right), -1)
    mine = [own_t, from_left, from_right, from_left2, from_right2]
    theirs = [other_core(piece) for piece in mine]
    rows_at = [
        zl,
        jnp.where(zl == 0, -1, zl - 1),
        jnp.where(zl == 3, -1, zl + 1),
        jnp.where(zl == 0, 3, jnp.where(zl == 1, -1, zl - 2)),
        jnp.where(zl == 3, 0, jnp.where(zl == 2, -1, zl + 2)),
    ]
    trace_meta = [jnp.where(at < 0, -1, at * 2 + core) for at in rows_at]
    trace_meta += [jnp.where(at < 0, -1, at * 2 + 1 - core) for at in rows_at]
    trace_meta = jnp.stack(meta_of(zh) + trace_meta).astype(jnp.int32)
    t_keep, t_send = pl.pallas_call(
        trace_kernel,
        grid_spec=pltpu.PrefetchScalarGridSpec(
            num_scalar_prefetch=3,
            grid=(4,),
            in_specs=[
                pl.BlockSpec((1, 8, 2, 2, 128, 256), lambda k, *_: (k, 0, 0, 0, 0, 0)),
                pl.BlockSpec((2, 8, 256), lambda k, *_: (0, 0, 0)),
            ]
            + [pl.BlockSpec((2, 8, 128, 128), lambda k, *_: (0, 0, 0, 0))] * 10,
            out_specs=[pl.BlockSpec((1, 8, 8, 128), lambda k, *_: (k, 0, 0, 0))] * 2,
            scratch_shapes=[pltpu.VMEM((128, 256), jnp.float32)],
        ),
        out_shape=[jax.ShapeDtypeStruct((4, 8, 8, 128), jnp.float32)] * 2,
        cost_estimate=pl.CostEstimate(flops=2 * 4 * 128 * 256 * 4096, bytes_accessed=14 * 2**20, transcendentals=0),
        compiler_params=pltpu.CompilerParams(vmem_limit_bytes=40 * 2**20),
        name="trace",
    )(trace_meta, pole_weights, pole_order, parts, diag_inverse, *mine, *theirs)

    density = keep + other_core(send)
    density = jnp.sum(lax.all_to_all(density, "pole", 0, 0), axis=0)

    def row_piece(at):
        return lax.dynamic_index_in_dim(density, at, 0, keepdims=False)

    got = [z_partner(row_piece(zl ^ bits), bits) for bits in (1, 2, 3)]
    density = row_piece(zl) + got[0] + got[1] + got[2]
    density = density * lax.dynamic_index_in_dim(ancestor_mask[0], y, 0, keepdims=False).astype(jnp.float32)

    diag = t_keep + other_core(t_send)

    def node_piece(at):
        return lax.dynamic_index_in_dim(diag, at % 4, 0, keepdims=False)

    got = [along_x(node_piece(xc + by), by) for by in (1, -1, 2)]
    diag = node_piece(xc) + got[0] + got[1] + got[2]
    groups = [[place(x, zz, cc) for zz in range(Z)] for x in range(X) for cc in range(C)]
    diag = jnp.sum(lax.all_to_all(diag, "blk", 0, 0, axis_index_groups=groups), axis=0)
    diag = diag.reshape(8, 4, 32).transpose(1, 0, 2)
    diag = jnp.sum(lax.all_to_all(diag, "pole", 0, 0), axis=0)
    return density, diag


def solution(mesh):
    placed = (
        P("pole", "blk", None),
        P("pole", "blk", None),
        P("blk", None),
        P("pole", "blk", None),
        P(),
        P(),
    )
    return jax.shard_map(
        per_device,
        mesh=mesh,
        in_specs=placed,
        out_specs=(P("blk", "pole"), P("blk", "pole")),
        check_vma=False,
    )
```

```python
import jax
import jax.numpy as jnp
from jax import lax
from jax.experimental import pallas as pl
from jax.experimental.pallas import tpu as pltpu
from jax.sharding import PartitionSpec as P

X, Z, C, Y = 4, 8, 2, 4
ROWS = 256
VMEM = pl.BlockSpec(memory_space=pltpu.VMEM)
SMEM = pl.BlockSpec(memory_space=pltpu.SMEM)
ANY = pl.BlockSpec(memory_space=pl.ANY)
HBM = pl.BlockSpec(memory_space=pltpu.HBM)
MIB = 2**20
NEAR_MIB, FAR_MIB, TRACE_MIB = 8, 10, 8


def place(x, z, core):
    return (x % X) * Z * C + (z % Z) * C + core


PLACES = [(x, z, core) for x in range(X) for z in range(Z) for core in range(C)]


def along_x(value, by):
    return lax.ppermute(value, "blk", [(place(*at), place(at[0] + by, at[1], at[2])) for at in PLACES])


def along_z(value, by):
    return lax.ppermute(value, "blk", [(place(*at), place(at[0], at[1] + by, at[2])) for at in PLACES])


def x_partner(value, bits):
    return lax.ppermute(value, "blk", [(place(*at), place(at[0] ^ bits, at[1], at[2])) for at in PLACES])


def z_partner(value, bits):
    return lax.ppermute(value, "blk", [(place(*at), place(at[0], at[1] ^ bits, at[2])) for at in PLACES])


def other_core(value):
    return lax.ppermute(value, "blk", [(place(*at), place(at[0], at[1], 1 - at[2])) for at in PLACES])


def opposite(value):
    return lax.ppermute(value, "blk", [(place(*at), place(at[0], at[1] ^ 4, 1 - at[2])) for at in PLACES])


def y_partner(value, bits):
    return lax.ppermute(value, "pole", [(y, y ^ bits) for y in range(Y)])


def coordinates():
    rank = lax.axis_index("blk")
    return lax.axis_index("pole"), rank >> 4, (rank >> 1) & 7, rank & 1


def columns_of(x, side):
    return [(((x + by) & 3) * 2 + side) * 256 for by in (0, 3, 1, 2)]


def mask_kernel(mask, order, weights, panel, own, factors):
    y, _, _, _ = coordinates()
    for k in range(4):
        for t in range(2):
            part = slice(t * 512 + k * 128, t * 512 + k * 128 + 128)
            value = panel[:, :, part]
            own[:, :, part] = jnp.where(mask[0, k] != 0, value, jnp.zeros_like(value))
    column = lax.broadcasted_iota(jnp.int32, (2, 8), 1)
    for p in range(2):
        chosen = jnp.where(column == order[y * 2 + p], weights[...], 0.0)
        factors[2 * p : 2 * p + 2, :] = jnp.broadcast_to(jnp.sum(chosen, axis=1, keepdims=True), (2, 512))


def build_form(form, panels):
    for step, panel_ref in enumerate(panels):
        top = step * 256
        form[top : top + 128, :] = panel_ref[...]
        form[top + 128 : top + 256, :512] = -panel_ref[:, 512:]
        form[top + 128 : top + 256, 512:] = panel_ref[:, :512]


def multiply(inverse, panels, form, columns, use):
    for p in range(2):
        build_form(form, [panel.at[p] for panel in panels])

        @pl.loop(0, 4)
        def _(tile):
            top = pl.multiple_of(tile * ROWS, ROWS)
            left = jnp.concatenate(
                [inverse[p, pl.ds(top, ROWS), pl.ds(pl.multiple_of(at, 256), 256)] for at in columns], axis=1
            )
            use(p, tile, jnp.dot(left, form[...], preferred_element_type=jnp.float32))


def first_kernel(inverse, own, right, left, across, out, form):
    _, x, z, _ = coordinates()

    def use(p, tile, value):
        out[p, pl.ds(pl.multiple_of(tile * ROWS, ROWS), ROWS), :] = value

    multiply(inverse, (own, right, left, across), form, columns_of(x, z >> 2), use)


def second_kernel(factors, inverse, before, own, right, left, across, token0, token1, keep, send, parts, form):
    y, x, z, core = coordinates()
    zl = z & 3

    def use(p, tile, value):
        w_re, w_im = factors[2 * p : 2 * p + 1, :], factors[2 * p + 1 : 2 * p + 2, :]
        total = before[p, pl.ds(pl.multiple_of(tile * ROWS, ROWS), ROWS), :] + value
        real, imag = total[:, :512], total[:, 512:]
        q_re = w_re * real - w_im * imag
        q_im = -(w_re * imag + w_im * real)
        near = tile ^ zl
        for k in range(4):
            for side, q in enumerate((q_re, q_im)):
                for c in range(2):
                    parts[k, tile * 2 + c, p, side] = q[c * 128 : c * 128 + 128, k * 128 : k * 128 + 128]
            even = q_re[:128, k * 128 : k * 128 + 128]
            odd = q_re[128:, k * 128 : k * 128 + 128]
            kept = jnp.where(core == 0, even, odd)
            sent = jnp.where(core == 0, odd, even)
            if p == 0:
                keep[k ^ y, near] = -kept
                send[k ^ y, near] = -sent
            else:
                keep[k ^ y, near] = keep[k ^ y, near] - kept
                send[k ^ y, near] = send[k ^ y, near] - sent

    multiply(inverse, (own, right, left, across), form, columns_of(x, 1 - (z >> 2)), use)


def flip_kernel(panel, token0, token1, token2, token3, out):
    for p in range(2):
        for part in range(8):
            out[p, part] = panel[p, :, part * 128 : part * 128 + 128].T


def hop_kernel(far, from_left, from_right, to_right, to_left):
    _, _, z, _ = coordinates()
    zl = z & 3
    for edge, got, out in ((3, from_left, to_right), (0, from_right, to_left)):
        @pl.when(zl == edge)
        def _():
            for p in range(2):
                for part in range(8):
                    out[p, part] = far[p, :, part * 128 : part * 128 + 128].T

        @pl.when(zl != edge)
        def _():
            out[...] = got[...]


def pair_kernel(keep, got, *outs):
    for bits in range(4):
        outs[bits][...] = keep[bits] + got[bits]


def add_kernel(a, b, c, d, *outs):
    for bits in range(4):
        outs[bits][...] = (a[bits] + b[bits]) + (c[bits] + d[bits])


def join_kernel(*refs):
    density, diag, outs = refs[:4], refs[4:8], refs[8:]
    small = (diag[0][...] + diag[1][...]) + (diag[2][...] + diag[3][...])
    for bits in range(4):
        outs[bits][:128] = (density[0][bits] + density[1][bits]) + (density[2][bits] + density[3][bits])
        outs[bits][128:] = small


def trace_kernel(factors, parts, diag, token, *rest):
    pieces, outs, total = rest[:10], rest[10:14], rest[14]
    y, x, z, core = coordinates()
    zl = z & 3
    total[...] = jnp.zeros_like(total)
    rows_at = [
        zl,
        jnp.where(zl == 0, -1, zl - 1),
        jnp.where(zl == 3, -1, zl + 1),
        jnp.where(zl == 0, 3, jnp.where(zl == 1, -1, zl - 2)),
        jnp.where(zl == 3, 0, jnp.where(zl == 2, -1, zl + 2)),
    ]
    for index, piece in enumerate(pieces):
        row = rows_at[index % 5]
        c = row * 2 + (core if index < 5 else 1 - core)

        @pl.when(row >= 0)
        def _():
            for k in range(4):
                left = jnp.concatenate(
                    [piece[p, side * 4 + k] for p in range(2) for side in range(2)], axis=1
                )
                right = parts[k, c].reshape(512, 128)
                high = right.astype(jnp.bfloat16)
                low = (right - high.astype(jnp.float32)).astype(jnp.bfloat16)
                total[k] += jnp.dot(
                    left, jnp.concatenate([high, low], axis=1), preferred_element_type=jnp.float32
                )

    mine = jnp.zeros((8, 128), jnp.float32)
    for p in range(2):
        w_re, w_im = factors[2 * p : 2 * p + 1, :128], factors[2 * p + 1 : 2 * p + 2, :128]
        mine += w_re * diag[p, :, :128] - w_im * diag[p, :, 128:]
    row = pl.multiple_of((z * 2 + core) * 8, 8)
    total[x, pl.ds(row, 8), :128] = total[x, pl.ds(row, 8), :128] + mine
    for k in range(4):
        value = (total[k, :, :128] + total[k, :, 128:]).T
        for target in range(4):
            piece = value[target * 32 : target * 32 + 32]
            for bits in range(4):
                @pl.when((y ^ bits) == target)
                def _():
                    outs[bits][k ^ x] = piece


def per_device(inverse_blocks, panel_blocks, ancestor_mask, diag_inverse, pole_weights, pole_order):
    y, xc, z, core = coordinates()
    zl = z & 3

    own, factors = pl.pallas_call(
        mask_kernel,
        in_specs=[SMEM] * 2 + [VMEM] * 2,
        out_specs=[VMEM] * 2,
        out_shape=[
            jax.ShapeDtypeStruct((2, 128, 1024), jnp.bfloat16),
            jax.ShapeDtypeStruct((4, 512), jnp.float32),
        ],
        cost_estimate=pl.CostEstimate(flops=0, bytes_accessed=MIB, transcendentals=0),
        compiler_params=pltpu.CompilerParams(vmem_limit_bytes=8 * MIB),
        name="mask",
    )(ancestor_mask, pole_order, pole_weights.T, panel_blocks)
    far = z_partner(own, 4)
    near_panels = [own, along_x(own, 1), along_x(own, -1), along_x(own, 2)]
    far_panels = [far, along_x(far, 1), along_x(far, -1), along_x(far, 2)]

    scratch = [pltpu.VMEM((1024, 1024), jnp.bfloat16)]
    inverse = inverse_blocks
    partial = pl.pallas_call(
        first_kernel,
        in_specs=[VMEM] * 5,
        out_specs=VMEM,
        scratch_shapes=scratch,
        out_shape=jax.ShapeDtypeStruct((2, 1024, 1024), jnp.float32),
        cost_estimate=pl.CostEstimate(flops=2 * 2 * 1024**3, bytes_accessed=4 * MIB, transcendentals=0),
        compiler_params=pltpu.CompilerParams(vmem_limit_bytes=NEAR_MIB * MIB),
        name="near",
    )(inverse, *near_panels)

    def flip(panel, *tokens):
        return pl.pallas_call(
            flip_kernel,
            in_specs=[VMEM] + [ANY] * 4,
            out_specs=VMEM,
            out_shape=jax.ShapeDtypeStruct((2, 8, 128, 128), jnp.bfloat16),
            cost_estimate=pl.CostEstimate(flops=0, bytes_accessed=MIB, transcendentals=0),
            compiler_params=pltpu.CompilerParams(vmem_limit_bytes=8 * MIB),
            name="flip",
        )(panel, *tokens)

    own_t = flip(own, far, *near_panels[1:])
    from_left, from_right = along_z(own_t, 1), along_z(own_t, -1)
    hops = pl.pallas_call(
        hop_kernel,
        in_specs=[VMEM] * 3,
        out_specs=[VMEM] * 2,
        out_shape=[jax.ShapeDtypeStruct((2, 8, 128, 128), jnp.bfloat16)] * 2,
        cost_estimate=pl.CostEstimate(flops=0, bytes_accessed=2 * MIB, transcendentals=0),
        compiler_params=pltpu.CompilerParams(vmem_limit_bytes=8 * MIB),
        name="hop",
    )(far, from_left, from_right)

    from_left2, from_right2 = along_z(hops[0], 1), along_z(hops[1], -1)

    keep, send, parts = pl.pallas_call(
        second_kernel,
        in_specs=[VMEM] * 7 + [ANY] * 2,
        out_specs=[VMEM] * 3,
        scratch_shapes=scratch,
        out_shape=[
            jax.ShapeDtypeStruct((4, 4, 128, 128), jnp.float32),
            jax.ShapeDtypeStruct((4, 4, 128, 128), jnp.float32),
            jax.ShapeDtypeStruct((4, 8, 2, 2, 128, 128), jnp.float32),
        ],
        cost_estimate=pl.CostEstimate(flops=2 * 2 * 1024**3, bytes_accessed=4 * MIB, transcendentals=0),
        compiler_params=pltpu.CompilerParams(vmem_limit_bytes=FAR_MIB * MIB),
        name="far",
    )(factors, inverse, partial, *far_panels, from_left2, from_right2)

    mine = [own_t, from_left, from_right, from_left2, from_right2]
    theirs = [other_core(piece) for piece in mine]

    def small(body, name, shape, *operands):
        return pl.pallas_call(
            body,
            in_specs=[VMEM] * len(operands),
            out_specs=[VMEM] * 4,
            out_shape=[jax.ShapeDtypeStruct(shape, jnp.float32)] * 4,
            cost_estimate=pl.CostEstimate(flops=0, bytes_accessed=MIB, transcendentals=0),
            compiler_params=pltpu.CompilerParams(vmem_limit_bytes=8 * MIB),
            name=name,
        )(*operands)

    density = small(pair_kernel, "pair", (4, 128, 128), keep, other_core(send))
    traces = pl.pallas_call(
        trace_kernel,
        in_specs=[VMEM] * 3 + [ANY] + [VMEM] * 10,
        out_specs=[VMEM] * 4,
        scratch_shapes=[pltpu.VMEM((4, 128, 256), jnp.float32)],
        out_shape=[jax.ShapeDtypeStruct((4, 32, 128), jnp.float32)] * 4,
        cost_estimate=pl.CostEstimate(flops=2 * 4 * 128 * 256 * 4096, bytes_accessed=4 * MIB, transcendentals=0),
        compiler_params=pltpu.CompilerParams(vmem_limit_bytes=TRACE_MIB * MIB),
        name="trace",
    )(factors, parts, diag_inverse, density[0], *mine, *theirs)

    density = [density[0]] + [y_partner(density[bits], bits) for bits in (1, 2, 3)]
    diag = [traces[0]] + [y_partner(traces[bits], bits) for bits in (1, 2, 3)]
    diag = small(add_kernel, "add", (32, 128), *diag)
    diag = [diag[0]] + [x_partner(diag[bits], bits) for bits in (1, 2, 3)]
    joint = small(join_kernel, "join", (160, 128), *density, *diag)
    joint = sum([z_partner(joint[bits], bits) for bits in (1, 2, 3)], joint[0])
    diag = joint[128:]
    density = joint[:128] * lax.dynamic_index_in_dim(ancestor_mask[0], y, 0, keepdims=False).astype(jnp.float32)
    diag = sum([z_partner(diag, 4), other_core(diag), opposite(diag)], diag)
    diag = lax.dynamic_slice_in_dim(diag, (z * 2 + core) * 8, 8, 1).T
    return density, diag


def solution(mesh):
    placed = (
        P("pole", "blk", None),
        P("pole", "blk", None),
        P("blk", None),
        P("pole", "blk", None),
        P(),
        P(),
    )
    return jax.shard_map(
        per_device,
        mesh=mesh,
        in_specs=placed,
        out_specs=(P("blk", "pole"), P("blk", "pole")),
        check_vma=False,
    )
```

```python
import jax
import jax.numpy as jnp
from jax import lax
from jax.experimental import pallas as pl
from jax.experimental.pallas import tpu as pltpu
from jax.sharding import PartitionSpec as P

X, Z, C, Y = 4, 8, 2, 4
ROWS = 512
VMEM = pl.BlockSpec(memory_space=pltpu.VMEM)
SMEM = pl.BlockSpec(memory_space=pltpu.SMEM)
ANY = pl.BlockSpec(memory_space=pl.ANY)
HBM = pl.BlockSpec(memory_space=pltpu.HBM)
MIB = 2**20
NEAR_MIB, FAR_MIB, TRACE_MIB = 8, 10, 8


def place(x, z, core):
    return (x % X) * Z * C + (z % Z) * C + core


PLACES = [(x, z, core) for x in range(X) for z in range(Z) for core in range(C)]


def along_x(value, by):
    return lax.ppermute(value, "blk", [(place(*at), place(at[0] + by, at[1], at[2])) for at in PLACES])


def along_z(value, by):
    return lax.ppermute(value, "blk", [(place(*at), place(at[0], at[1] + by, at[2])) for at in PLACES])


def x_partner(value, bits):
    return lax.ppermute(value, "blk", [(place(*at), place(at[0] ^ bits, at[1], at[2])) for at in PLACES])


def z_partner(value, bits):
    return lax.ppermute(value, "blk", [(place(*at), place(at[0], at[1] ^ bits, at[2])) for at in PLACES])


def other_core(value):
    return lax.ppermute(value, "blk", [(place(*at), place(at[0], at[1], 1 - at[2])) for at in PLACES])


def y_partner(value, bits):
    return lax.ppermute(value, "pole", [(y, y ^ bits) for y in range(Y)])


def coordinates():
    rank = lax.axis_index("blk")
    return lax.axis_index("pole"), rank >> 4, (rank >> 1) & 7, rank & 1


def columns_of(x, side):
    return [(((x + by) & 3) * 2 + side) * 256 for by in (0, 3, 1, 2)]


def mask_kernel(mask, panel, own):
    for k in range(4):
        for t in range(2):
            part = slice(t * 512 + k * 128, t * 512 + k * 128 + 128)
            value = panel[:, :, part]
            own[:, :, part] = jnp.where(mask[0, k] != 0, value, jnp.zeros_like(value))


def factor_kernel(order, weights, token, factors):
    y, _, _, _ = coordinates()
    column = lax.broadcasted_iota(jnp.int32, (2, 8), 1)
    for p in range(2):
        chosen = jnp.where(column == order[y * 2 + p], weights[...], 0.0)
        factors[2 * p : 2 * p + 2, :] = jnp.broadcast_to(jnp.sum(chosen, axis=1, keepdims=True), (2, 512))


def build_form(form, panels):
    for step, panel_ref in enumerate(panels):
        top = step * 256
        form[top : top + 128, :] = panel_ref[...]
        form[top + 128 : top + 256, :512] = -panel_ref[:, 512:]
        form[top + 128 : top + 256, 512:] = panel_ref[:, :512]


def multiply(inverse, panels, form, columns, use):
    for p in range(2):
        build_form(form, [panel.at[p] for panel in panels])

        @pl.loop(0, 1024 // ROWS)
        def _(tile):
            top = pl.multiple_of(tile * ROWS, ROWS)
            left = jnp.concatenate(
                [inverse[p, pl.ds(top, ROWS), pl.ds(pl.multiple_of(at, 256), 256)] for at in columns], axis=1
            )
            use(p, tile, jnp.dot(left, form[...], preferred_element_type=jnp.float32))


def first_kernel(inverse, own, right, left, across, out, form):
    _, x, z, _ = coordinates()

    def use(p, tile, value):
        out[p, pl.ds(pl.multiple_of(tile * ROWS, ROWS), ROWS), :] = value

    multiply(inverse, (own, right, left, across), form, columns_of(x, z >> 2), use)


def second_kernel(factors, inverse, before, own, right, left, across, *rest):
    keep, send, parts, form = rest[-4:]
    y, x, z, core = coordinates()
    zl = z & 3

    def use(p, tile, value):
        w_re, w_im = factors[2 * p : 2 * p + 1, :], factors[2 * p + 1 : 2 * p + 2, :]
        total = before[p, pl.ds(pl.multiple_of(tile * ROWS, ROWS), ROWS), :] + value
        real, imag = total[:, :512], total[:, 512:]
        q_re = w_re * real - w_im * imag
        q_im = -(w_re * imag + w_im * real)
        for k in range(4):
            part = slice(k * 128, k * 128 + 128)
            for c in range(ROWS // 128):
                for side, q in enumerate((q_re, q_im)):
                    parts[k, tile * (ROWS // 128) + c, p, side] = q[c * 128 : c * 128 + 128, part]
            for pair in range(ROWS // 256):
                near = (tile * (ROWS // 256) + pair) ^ zl
                even = q_re[pair * 256 : pair * 256 + 128, part]
                odd = q_re[pair * 256 + 128 : pair * 256 + 256, part]
                kept = jnp.where(core == 0, even, odd)
                sent = jnp.where(core == 0, odd, even)
                if p == 0:
                    keep[k ^ y, near] = -kept
                    send[k ^ y, near] = -sent
                else:
                    keep[k ^ y, near] = keep[k ^ y, near] - kept
                    send[k ^ y, near] = send[k ^ y, near] - sent

    multiply(inverse, (own, right, left, across), form, columns_of(x, 1 - (z >> 2)), use)


def flip_kernel(panel, token0, token1, token2, token3, out):
    for p in range(2):
        for part in range(8):
            out[p, part] = panel[p, :, part * 128 : part * 128 + 128].T


def hop_kernel(far, from_left, from_right, to_right, to_left):
    _, _, z, _ = coordinates()
    zl = z & 3
    for edge, got, out in ((3, from_left, to_right), (0, from_right, to_left)):
        @pl.when(zl == edge)
        def _():
            for p in range(2):
                for part in range(8):
                    out[p, part] = far[p, :, part * 128 : part * 128 + 128].T

        @pl.when(zl != edge)
        def _():
            out[...] = got[...]


def pair_kernel(keep, got, *outs):
    for bits in range(4):
        outs[bits][...] = keep[bits] + got[bits]


def add_kernel(a, b, c, d, *outs):
    y, _, _, _ = coordinates()
    total = (a[...] + b[...]) + (c[...] + d[...])
    for target in range(4):
        for bits in range(4):
            @pl.when((y ^ bits) == target)
            def _():
                outs[bits][...] = total[target * 32 : target * 32 + 32]


def join_kernel(*refs):
    density, diag, outs = refs[:4], refs[4:8], refs[8:]
    small = (diag[0][...] + diag[1][...]) + (diag[2][...] + diag[3][...])
    for bits in range(4):
        outs[bits][:128] = (density[0][bits] + density[1][bits]) + (density[2][bits] + density[3][bits])
        outs[bits][128:] = small


def trace_kernel(factors, parts, diag, *rest):
    pieces, out, total = rest[:10], rest[10], rest[11]
    y, x, z, core = coordinates()
    zl = z & 3
    total[...] = jnp.zeros_like(total)
    rows_at = [
        zl,
        jnp.where(zl == 0, -1, zl - 1),
        jnp.where(zl == 3, -1, zl + 1),
        jnp.where(zl == 0, 3, jnp.where(zl == 1, -1, zl - 2)),
        jnp.where(zl == 3, 0, jnp.where(zl == 2, -1, zl + 2)),
    ]
    for index, piece in enumerate(pieces):
        row = rows_at[index % 5]
        c = row * 2 + (core if index < 5 else 1 - core)

        @pl.when(row >= 0)
        def _():
            for k in range(4):
                left = jnp.concatenate(
                    [piece[p, side * 4 + k] for p in range(2) for side in range(2)], axis=1
                )
                right = parts[k, c].reshape(512, 128)
                high = right.astype(jnp.bfloat16)
                low = (right - high.astype(jnp.float32)).astype(jnp.bfloat16)
                total[k] += jnp.dot(
                    left, jnp.concatenate([high, low], axis=1), preferred_element_type=jnp.float32
                )

    mine = jnp.zeros((8, 128), jnp.float32)
    for p in range(2):
        w_re, w_im = factors[2 * p : 2 * p + 1, :128], factors[2 * p + 1 : 2 * p + 2, :128]
        mine += w_re * diag[p, :, :128] - w_im * diag[p, :, 128:]
    row = pl.multiple_of((z * 2 + core) * 8, 8)
    total[x, pl.ds(row, 8), :128] = total[x, pl.ds(row, 8), :128] + mine
    for k in range(4):
        out[k ^ x] = (total[k, :, :128] + total[k, :, 128:]).T


def per_device(inverse_blocks, panel_blocks, ancestor_mask, diag_inverse, pole_weights, pole_order):
    y, xc, z, core = coordinates()
    zl = z & 3

    own = pl.pallas_call(
        mask_kernel,
        in_specs=[SMEM, VMEM],
        out_specs=VMEM,
        out_shape=jax.ShapeDtypeStruct((2, 128, 1024), jnp.bfloat16),
        cost_estimate=pl.CostEstimate(flops=0, bytes_accessed=MIB, transcendentals=0),
        compiler_params=pltpu.CompilerParams(vmem_limit_bytes=8 * MIB),
        name="mask",
    )(ancestor_mask, panel_blocks)
    factors = pl.pallas_call(
        factor_kernel,
        in_specs=[SMEM, VMEM, ANY],
        out_specs=VMEM,
        out_shape=jax.ShapeDtypeStruct((4, 512), jnp.float32),
        cost_estimate=pl.CostEstimate(flops=0, bytes_accessed=8192, transcendentals=0),
        compiler_params=pltpu.CompilerParams(vmem_limit_bytes=8 * MIB),
        name="factors",
    )(pole_order, pole_weights.T, own)
    far = z_partner(own, 4)
    near_panels = [own, along_x(own, 1), along_x(own, -1), along_x(own, 2)]
    far_panels = [far, along_x(far, 1), along_x(far, -1), along_x(far, 2)]

    scratch = [pltpu.VMEM((1024, 1024), jnp.bfloat16)]
    inverse = inverse_blocks
    partial = pl.pallas_call(
        first_kernel,
        in_specs=[VMEM] * 5,
        out_specs=VMEM,
        scratch_shapes=scratch,
        out_shape=jax.ShapeDtypeStruct((2, 1024, 1024), jnp.float32),
        cost_estimate=pl.CostEstimate(flops=2 * 2 * 1024**3, bytes_accessed=4 * MIB, transcendentals=0),
        compiler_params=pltpu.CompilerParams(vmem_limit_bytes=NEAR_MIB * MIB),
        name="near",
    )(inverse, *near_panels)

    def flip(panel, *tokens):
        return pl.pallas_call(
            flip_kernel,
            in_specs=[VMEM] + [ANY] * 4,
            out_specs=VMEM,
            out_shape=jax.ShapeDtypeStruct((2, 8, 128, 128), jnp.bfloat16),
            cost_estimate=pl.CostEstimate(flops=0, bytes_accessed=MIB, transcendentals=0),
            compiler_params=pltpu.CompilerParams(vmem_limit_bytes=8 * MIB),
            name="flip",
        )(panel, *tokens)

    own_t = flip(own, far, *near_panels[1:])
    from_left, from_right = along_z(own_t, 1), along_z(own_t, -1)
    hops = pl.pallas_call(
        hop_kernel,
        in_specs=[VMEM] * 3,
        out_specs=[VMEM] * 2,
        out_shape=[jax.ShapeDtypeStruct((2, 8, 128, 128), jnp.bfloat16)] * 2,
        cost_estimate=pl.CostEstimate(flops=0, bytes_accessed=2 * MIB, transcendentals=0),
        compiler_params=pltpu.CompilerParams(vmem_limit_bytes=8 * MIB),
        name="hop",
    )(far, from_left, from_right)

    from_left2, from_right2 = along_z(hops[0], 1), along_z(hops[1], -1)
    theirs = [other_core(piece) for piece in (own_t, from_left, from_right)]

    keep, send, parts = pl.pallas_call(
        second_kernel,
        in_specs=[VMEM] * 7 + [ANY] * 3,
        out_specs=[VMEM] * 3,
        scratch_shapes=scratch,
        out_shape=[
            jax.ShapeDtypeStruct((4, 4, 128, 128), jnp.float32),
            jax.ShapeDtypeStruct((4, 4, 128, 128), jnp.float32),
            jax.ShapeDtypeStruct((4, 8, 2, 2, 128, 128), jnp.float32),
        ],
        cost_estimate=pl.CostEstimate(flops=2 * 2 * 1024**3, bytes_accessed=4 * MIB, transcendentals=0),
        compiler_params=pltpu.CompilerParams(vmem_limit_bytes=FAR_MIB * MIB),
        name="far",
    )(factors, inverse, partial, *far_panels, from_left2, from_right2, theirs[0])

    mine = [own_t, from_left, from_right, from_left2, from_right2]
    theirs = theirs + [other_core(piece) for piece in mine[3:]]

    def small(body, name, shape, *operands):
        return pl.pallas_call(
            body,
            in_specs=[VMEM] * len(operands),
            out_specs=[VMEM] * 4,
            out_shape=[jax.ShapeDtypeStruct(shape, jnp.float32)] * 4,
            cost_estimate=pl.CostEstimate(flops=0, bytes_accessed=MIB, transcendentals=0),
            compiler_params=pltpu.CompilerParams(vmem_limit_bytes=8 * MIB),
            name=name,
        )(*operands)

    density = small(pair_kernel, "pair", (4, 128, 128), keep, other_core(send))
    traces = pl.pallas_call(
        trace_kernel,
        in_specs=[VMEM] * 13,
        out_specs=VMEM,
        scratch_shapes=[pltpu.VMEM((4, 128, 256), jnp.float32)],
        out_shape=jax.ShapeDtypeStruct((4, 128, 128), jnp.float32),
        cost_estimate=pl.CostEstimate(flops=2 * 4 * 128 * 256 * 4096, bytes_accessed=4 * MIB, transcendentals=0),
        compiler_params=pltpu.CompilerParams(vmem_limit_bytes=TRACE_MIB * MIB),
        name="trace",
    )(factors, parts, diag_inverse, *mine, *theirs)
    diag = small(pair_kernel, "cores", (128, 128), traces, other_core(traces))
    density = [density[0]] + [y_partner(density[bits], bits) for bits in (1, 2, 3)]
    diag = small(add_kernel, "nodes", (32, 128), diag[0], *[x_partner(diag[bits], bits) for bits in (1, 2, 3)])
    diag = [diag[0]] + [y_partner(diag[bits], bits) for bits in (1, 2, 3)]
    joint = small(join_kernel, "join", (160, 128), *density, *diag)
    joint = sum([z_partner(joint[bits], bits) for bits in (1, 2, 3)], joint[0])
    diag = joint[128:]
    density = joint[:128] * lax.dynamic_index_in_dim(ancestor_mask[0], y, 0, keepdims=False).astype(jnp.float32)
    diag = diag + z_partner(diag, 4)
    diag = lax.dynamic_slice_in_dim(diag, (z * 2 + core) * 8, 8, 1).T
    return density, diag


def solution(mesh):
    placed = (
        P("pole", "blk", None),
        P("pole", "blk", None),
        P("blk", None),
        P("pole", "blk", None),
        P(),
        P(),
    )
    return jax.shard_map(
        per_device,
        mesh=mesh,
        in_specs=placed,
        out_specs=(P("blk", "pole"), P("blk", "pole")),
        check_vma=False,
    )
```

```python
import jax
import jax.numpy as jnp
from jax import lax
from jax.experimental import pallas as pl
from jax.experimental.pallas import tpu as pltpu
from jax.sharding import PartitionSpec as P

X, Z, C, Y = 4, 8, 2, 4
ROWS = 512
VMEM = pl.BlockSpec(memory_space=pltpu.VMEM)
SMEM = pl.BlockSpec(memory_space=pltpu.SMEM)
ANY = pl.BlockSpec(memory_space=pl.ANY)
HBM = pl.BlockSpec(memory_space=pltpu.HBM)
MIB = 2**20
NEAR_MIB, FAR_MIB, TRACE_MIB = 8, 10, 8


def place(x, z, core):
    return (x % X) * Z * C + (z % Z) * C + core


PLACES = [(x, z, core) for x in range(X) for z in range(Z) for core in range(C)]


def along_x(value, by):
    return lax.ppermute(value, "blk", [(place(*at), place(at[0] + by, at[1], at[2])) for at in PLACES])


def along_z(value, by):
    return lax.ppermute(value, "blk", [(place(*at), place(at[0], at[1] + by, at[2])) for at in PLACES])


def x_partner(value, bits):
    return lax.ppermute(value, "blk", [(place(*at), place(at[0] ^ bits, at[1], at[2])) for at in PLACES])


def z_partner(value, bits):
    return lax.ppermute(value, "blk", [(place(*at), place(at[0], at[1] ^ bits, at[2])) for at in PLACES])


def other_core(value):
    return lax.ppermute(value, "blk", [(place(*at), place(at[0], at[1], 1 - at[2])) for at in PLACES])


def y_partner(value, bits):
    return lax.ppermute(value, "pole", [(y, y ^ bits) for y in range(Y)])


def coordinates():
    rank = lax.axis_index("blk")
    return lax.axis_index("pole"), rank >> 4, (rank >> 1) & 7, rank & 1


def columns_of(x, side):
    return [(((x + by) & 3) * 2 + side) * 256 for by in (0, 3, 1, 2)]


def mask_kernel(mask, panel, own):
    for k in range(4):
        for t in range(2):
            part = slice(t * 512 + k * 128, t * 512 + k * 128 + 128)
            value = panel[:, :, part]
            own[:, :, part] = jnp.where(mask[0, k] != 0, value, jnp.zeros_like(value))


def factor_kernel(order, weights, token, factors):
    y, _, _, _ = coordinates()
    column = lax.broadcasted_iota(jnp.int32, (2, 8), 1)
    for p in range(2):
        chosen = jnp.where(column == order[y * 2 + p], weights[...], 0.0)
        factors[2 * p : 2 * p + 2, :] = jnp.broadcast_to(jnp.sum(chosen, axis=1, keepdims=True), (2, 512))


def build_form(form, panels):
    for step, panel_ref in enumerate(panels):
        top = step * 256
        form[top : top + 128, :] = panel_ref[...]
        form[top + 128 : top + 256, :512] = -panel_ref[:, 512:]
        form[top + 128 : top + 256, 512:] = panel_ref[:, :512]


def multiply(inverse, panels, form, columns, use):
    for p in range(2):
        build_form(form, panels[p])

        @pl.loop(0, 1024 // ROWS)
        def _(tile):
            top = pl.multiple_of(tile * ROWS, ROWS)
            left = jnp.concatenate(
                [inverse[p, pl.ds(top, ROWS), pl.ds(pl.multiple_of(at, 256), 256)] for at in columns], axis=1
            )
            use(p, tile, jnp.dot(left, form[...], preferred_element_type=jnp.float32))


def first_kernel(inverse, own, right, left, across, *rest):
    out, form = rest[-2:]
    _, x, z, _ = coordinates()

    def use(p, tile, value):
        out[p, pl.ds(pl.multiple_of(tile * ROWS, ROWS), ROWS), :] = value

    panels = [[panel.at[p] for panel in (own, right, left, across)] for p in range(2)]
    multiply(inverse, panels, form, columns_of(x, z >> 2), use)


def second_kernel(factors, inverse, before, own, right, left, across0, across1, keep, send, parts, form):
    across = (across0, across1)
    y, x, z, core = coordinates()
    zl = z & 3

    def use(p, tile, value):
        w_re, w_im = factors[2 * p : 2 * p + 1, :], factors[2 * p + 1 : 2 * p + 2, :]
        total = before[p, pl.ds(pl.multiple_of(tile * ROWS, ROWS), ROWS), :] + value
        real, imag = total[:, :512], total[:, 512:]
        q_re = w_re * real - w_im * imag
        q_im = -(w_re * imag + w_im * real)
        for k in range(4):
            part = slice(k * 128, k * 128 + 128)
            for c in range(ROWS // 128):
                for side, q in enumerate((q_re, q_im)):
                    parts[k, tile * (ROWS // 128) + c, p, side] = q[c * 128 : c * 128 + 128, part]
            for pair in range(ROWS // 256):
                near = (tile * (ROWS // 256) + pair) ^ zl
                even = q_re[pair * 256 : pair * 256 + 128, part]
                odd = q_re[pair * 256 + 128 : pair * 256 + 256, part]
                kept = jnp.where(core == 0, even, odd)
                sent = jnp.where(core == 0, odd, even)
                if p == 0:
                    keep[k ^ y, near] = -kept
                    send[k ^ y, near] = -sent
                else:
                    keep[k ^ y, near] = keep[k ^ y, near] - kept
                    send[k ^ y, near] = send[k ^ y, near] - sent

    panels = [[own.at[p], right.at[p], left.at[p], across[p]] for p in range(2)]
    multiply(inverse, panels, form, columns_of(x, 1 - (z >> 2)), use)


def flip_kernel(panel, token0, token1, token2, token3, token4, out):
    for p in range(2):
        for part in range(8):
            out[p, part] = panel[p, :, part * 128 : part * 128 + 128].T


def hop_kernel(far, from_left, from_right, right, left, to_right, to_left, relay_right, relay_left):
    _, _, z, _ = coordinates()
    zl = z & 3
    relay_right[...] = right[0]
    relay_left[...] = left[1]
    for edge, got, out in ((3, from_left, to_right), (0, from_right, to_left)):
        @pl.when(zl == edge)
        def _():
            for p in range(2):
                for part in range(8):
                    out[p, part] = far[p, :, part * 128 : part * 128 + 128].T

        @pl.when(zl != edge)
        def _():
            out[...] = got[...]


def gate_kernel(value, token0, token1, out):
    pass


def pair_kernel(keep, got, *rest):
    outs = rest[-4:]
    for bits in range(4):
        outs[bits][...] = keep[bits] + got[bits]


def add_kernel(a, b, *outs):
    y, _, _, _ = coordinates()
    total = a[...] + b[...]
    for target in range(4):
        for bits in range(4):
            @pl.when((y ^ bits) == target)
            def _():
                outs[bits][...] = total[target * 32 : target * 32 + 32]


def join_kernel(*refs):
    density, diag, outs = refs[:4], refs[4:8], refs[8:]
    small = (diag[0][...] + diag[1][...]) + (diag[2][...] + diag[3][...])
    for bits in range(4):
        outs[bits][:128] = (density[0][bits] + density[1][bits]) + (density[2][bits] + density[3][bits])
        outs[bits][128:] = small


def trace_kernel(factors, parts, diag, *rest):
    pieces, out, total = rest[:10], rest[10], rest[11]
    y, x, z, core = coordinates()
    zl = z & 3
    total[...] = jnp.zeros_like(total)
    rows_at = [
        zl,
        jnp.where(zl == 0, -1, zl - 1),
        jnp.where(zl == 3, -1, zl + 1),
        jnp.where(zl == 0, 3, jnp.where(zl == 1, -1, zl - 2)),
        jnp.where(zl == 3, 0, jnp.where(zl == 2, -1, zl + 2)),
    ]
    for index, piece in enumerate(pieces):
        row = rows_at[index % 5]
        c = row * 2 + (core if index < 5 else 1 - core)

        @pl.when(row >= 0)
        def _():
            for k in range(4):
                left = jnp.concatenate(
                    [piece[p, side * 4 + k] for p in range(2) for side in range(2)], axis=1
                )
                right = parts[k, c].reshape(512, 128)
                high = right.astype(jnp.bfloat16)
                low = (right - high.astype(jnp.float32)).astype(jnp.bfloat16)
                total[k] += jnp.dot(
                    left, jnp.concatenate([high, low], axis=1), preferred_element_type=jnp.float32
                )

    mine = jnp.zeros((8, 128), jnp.float32)
    for p in range(2):
        w_re, w_im = factors[2 * p : 2 * p + 1, :128], factors[2 * p + 1 : 2 * p + 2, :128]
        mine += w_re * diag[p, :, :128] - w_im * diag[p, :, 128:]
    row = pl.multiple_of((z * 2 + core) * 8, 8)
    total[x, pl.ds(row, 8), :128] = total[x, pl.ds(row, 8), :128] + mine
    for k in range(4):
        out[k ^ x] = (total[k, :, :128] + total[k, :, 128:]).T


def per_device(inverse_blocks, panel_blocks, ancestor_mask, diag_inverse, pole_weights, pole_order):
    y, xc, z, core = coordinates()
    zl = z & 3

    own = pl.pallas_call(
        mask_kernel,
        in_specs=[SMEM, VMEM],
        out_specs=VMEM,
        out_shape=jax.ShapeDtypeStruct((2, 128, 1024), jnp.bfloat16),
        cost_estimate=pl.CostEstimate(flops=0, bytes_accessed=MIB, transcendentals=0),
        compiler_params=pltpu.CompilerParams(vmem_limit_bytes=8 * MIB),
        name="mask",
    )(ancestor_mask, panel_blocks)
    factors = pl.pallas_call(
        factor_kernel,
        in_specs=[SMEM, VMEM, ANY],
        out_specs=VMEM,
        out_shape=jax.ShapeDtypeStruct((4, 512), jnp.float32),
        cost_estimate=pl.CostEstimate(flops=0, bytes_accessed=8192, transcendentals=0),
        compiler_params=pltpu.CompilerParams(vmem_limit_bytes=8 * MIB),
        name="factors",
    )(pole_order, pole_weights.T, own)
    far = z_partner(own, 4)
    near_panels = [own, along_x(own, 1), along_x(own, -1), along_x(own, 2)]
    far_right, far_left = along_x(far, 1), along_x(far, -1)

    scratch = [pltpu.VMEM((1024, 1024), jnp.bfloat16)]
    inverse = inverse_blocks
    def flip(panel, *tokens):
        return pl.pallas_call(
            flip_kernel,
            in_specs=[VMEM] + [ANY] * 5,
            out_specs=VMEM,
            out_shape=jax.ShapeDtypeStruct((2, 8, 128, 128), jnp.bfloat16),
            cost_estimate=pl.CostEstimate(flops=0, bytes_accessed=MIB, transcendentals=0),
            compiler_params=pltpu.CompilerParams(vmem_limit_bytes=8 * MIB),
            name="flip",
        )(panel, *tokens)

    own_t = flip(own, far, *near_panels[1:], factors)
    from_left, from_right = along_z(own_t, 1), along_z(own_t, -1)
    to_right, to_left, relay_right, relay_left = pl.pallas_call(
        hop_kernel,
        in_specs=[VMEM] * 5,
        out_specs=[VMEM] * 4,
        out_shape=[jax.ShapeDtypeStruct((2, 8, 128, 128), jnp.bfloat16)] * 2
        + [jax.ShapeDtypeStruct((128, 1024), jnp.bfloat16)] * 2,
        cost_estimate=pl.CostEstimate(flops=0, bytes_accessed=2 * MIB, transcendentals=0),
        compiler_params=pltpu.CompilerParams(vmem_limit_bytes=8 * MIB),
        name="hop",
    )(far, from_left, from_right, far_right, far_left)
    from_left2, from_right2 = along_z(to_right, 1), along_z(to_left, -1)
    far_panels = [far, far_right, far_left, along_x(relay_right, 1), along_x(relay_left, -1)]
    theirs = [other_core(piece) for piece in (own_t, from_left, from_right)]

    partial = pl.pallas_call(
        first_kernel,
        in_specs=[VMEM] * 5 + [ANY] * 3,
        out_specs=VMEM,
        scratch_shapes=scratch,
        out_shape=jax.ShapeDtypeStruct((2, 1024, 1024), jnp.float32),
        cost_estimate=pl.CostEstimate(flops=2 * 2 * 1024**3, bytes_accessed=4 * MIB, transcendentals=0),
        compiler_params=pltpu.CompilerParams(vmem_limit_bytes=NEAR_MIB * MIB),
        name="near",
    )(inverse, *near_panels, *theirs)

    keep, send, parts = pl.pallas_call(
        second_kernel,
        in_specs=[VMEM] * 8,
        out_specs=[VMEM] * 3,
        scratch_shapes=scratch,
        out_shape=[
            jax.ShapeDtypeStruct((4, 4, 128, 128), jnp.float32),
            jax.ShapeDtypeStruct((4, 4, 128, 128), jnp.float32),
            jax.ShapeDtypeStruct((4, 8, 2, 2, 128, 128), jnp.float32),
        ],
        cost_estimate=pl.CostEstimate(flops=0, bytes_accessed=0, transcendentals=0),
        compiler_params=pltpu.CompilerParams(vmem_limit_bytes=FAR_MIB * MIB),
        name="far",
    )(factors, inverse, partial, *far_panels)

    mine = [own_t, from_left, from_right, from_left2, from_right2]
    theirs = theirs + [other_core(piece) for piece in mine[3:]]

    def small(body, name, shape, *operands):
        return pl.pallas_call(
            body,
            in_specs=([VMEM] * 2 + [ANY]) if len(operands) == 3 else [VMEM] * len(operands),
            out_specs=[VMEM] * 4,
            out_shape=[jax.ShapeDtypeStruct(shape, jnp.float32)] * 4,
            cost_estimate=pl.CostEstimate(flops=0, bytes_accessed=MIB, transcendentals=0),
            compiler_params=pltpu.CompilerParams(vmem_limit_bytes=8 * MIB),
            name=name,
        )(*operands)

    send = pl.pallas_call(
        gate_kernel,
        in_specs=[ANY] * 3,
        out_specs=ANY,
        out_shape=jax.ShapeDtypeStruct((4, 4, 128, 128), jnp.float32),
        input_output_aliases={0: 0},
        cost_estimate=pl.CostEstimate(flops=0, bytes_accessed=0, transcendentals=0),
        compiler_params=pltpu.CompilerParams(vmem_limit_bytes=MIB),
        name="gate",
    )(send, from_left2, from_right2)
    density = small(pair_kernel, "pair", (4, 128, 128), keep, other_core(send))
    traces = pl.pallas_call(
        trace_kernel,
        in_specs=[VMEM] * 13,
        out_specs=VMEM,
        scratch_shapes=[pltpu.VMEM((4, 128, 256), jnp.float32)],
        out_shape=jax.ShapeDtypeStruct((4, 128, 128), jnp.float32),
        cost_estimate=pl.CostEstimate(flops=2 * 4 * 128 * 256 * 4096, bytes_accessed=4 * MIB, transcendentals=0),
        compiler_params=pltpu.CompilerParams(vmem_limit_bytes=TRACE_MIB * MIB),
        name="trace",
    )(factors, parts, diag_inverse, *mine, *theirs)
    diag = small(pair_kernel, "cores", (128, 128), traces, other_core(traces), density[0])
    density = [density[0]] + [y_partner(density[bits], bits) for bits in (1, 2, 3)]
    diag = sum([x_partner(diag[bits], bits) for bits in (1, 2, 3)], diag[0])
    halves = [diag, z_partner(diag, 4)]
    diag = small(add_kernel, "nodes", (32, 128), *halves)
    diag = [diag[0]] + [y_partner(diag[bits], bits) for bits in (1, 2, 3)]
    joint = small(join_kernel, "join", (160, 128), *density, *diag)
    joint = sum([z_partner(joint[bits], bits) for bits in (1, 2, 3)], joint[0])
    diag = joint[128:]
    density = joint[:128] * lax.dynamic_index_in_dim(ancestor_mask[0], y, 0, keepdims=False).astype(jnp.float32)
    diag = lax.dynamic_slice_in_dim(diag, (z * 2 + core) * 8, 8, 1).T
    return density, diag


def solution(mesh):
    placed = (
        P("pole", "blk", None),
        P("pole", "blk", None),
        P("blk", None),
        P("pole", "blk", None),
        P(),
        P(),
    )
    return jax.shard_map(
        per_device,
        mesh=mesh,
        in_specs=placed,
        out_specs=(P("blk", "pole"), P("blk", "pole")),
        check_vma=False,
    )
```

```python
import jax
import jax.numpy as jnp
from jax import lax
from jax.experimental import pallas as pl
from jax.experimental.pallas import tpu as pltpu
from jax.sharding import PartitionSpec as P

X, Z, C, Y = 4, 8, 2, 4
ROWS = 512
VMEM = pl.BlockSpec(memory_space=pltpu.VMEM)
SMEM = pl.BlockSpec(memory_space=pltpu.SMEM)
ANY = pl.BlockSpec(memory_space=pl.ANY)
HBM = pl.BlockSpec(memory_space=pltpu.HBM)
MIB = 2**20
NEAR_MIB, FAR_MIB, TRACE_MIB = 8, 10, 8


def place(x, z, core):
    return (x % X) * Z * C + (z % Z) * C + core


PLACES = [(x, z, core) for x in range(X) for z in range(Z) for core in range(C)]


def along_x(value, by):
    return lax.ppermute(value, "blk", [(place(*at), place(at[0] + by, at[1], at[2])) for at in PLACES])


def along_z(value, by):
    return lax.ppermute(value, "blk", [(place(*at), place(at[0], at[1] + by, at[2])) for at in PLACES])


def x_partner(value, bits):
    return lax.ppermute(value, "blk", [(place(*at), place(at[0] ^ bits, at[1], at[2])) for at in PLACES])


def z_partner(value, bits):
    return lax.ppermute(value, "blk", [(place(*at), place(at[0], at[1] ^ bits, at[2])) for at in PLACES])


def z_mirror(value):
    return lax.ppermute(value, "blk", [(place(*at), place(at[0], 7 - at[1], at[2])) for at in PLACES])


def other_core(value):
    return lax.ppermute(value, "blk", [(place(*at), place(at[0], at[1], 1 - at[2])) for at in PLACES])


def y_partner(value, bits):
    return lax.ppermute(value, "pole", [(y, y ^ bits) for y in range(Y)])


def coordinates():
    rank = lax.axis_index("blk")
    return lax.axis_index("pole"), rank >> 4, (rank >> 1) & 7, rank & 1


def columns_of(x, side):
    return [(((x + by) & 3) * 2 + side) * 256 for by in (0, 3, 1, 2)]


def mask_kernel(mask, panel, own):
    for k in range(4):
        for t in range(2):
            part = slice(t * 512 + k * 128, t * 512 + k * 128 + 128)
            value = panel[:, :, part]
            own[:, :, part] = jnp.where(mask[0, k] != 0, value, jnp.zeros_like(value))


def factor_kernel(order, weights, token, factors):
    y, _, _, _ = coordinates()
    column = lax.broadcasted_iota(jnp.int32, (2, 8), 1)
    for p in range(2):
        chosen = jnp.where(column == order[y * 2 + p], weights[...], 0.0)
        factors[2 * p : 2 * p + 2, :] = jnp.broadcast_to(jnp.sum(chosen, axis=1, keepdims=True), (2, 512))


def build_form(form, panels):
    for step, panel_ref in enumerate(panels):
        top = step * 256
        form[top : top + 128, :] = panel_ref[...]
        form[top + 128 : top + 256, :512] = -panel_ref[:, 512:]
        form[top + 128 : top + 256, 512:] = panel_ref[:, :512]


def load_kernel(inverse, token, out, sems):
    copies = [
        pltpu.make_async_copy(
            inverse.at[p, pl.ds(half * 512, 512)], out.at[p, pl.ds(half * 512, 512)], sems.at[p, half]
        )
        for p in range(2)
        for half in range(2)
    ]
    for copy in copies:
        copy.start()
    for copy in copies:
        copy.wait()


def relay_kernel(right, left, relay_right, relay_left):
    relay_right[...] = right[0]
    relay_left[...] = left[1]


def multiply(inverse, panels, form, columns, use):
    for p in range(2):
        build_form(form, panels[p])

        @pl.loop(0, 1024 // ROWS)
        def _(tile):
            top = pl.multiple_of(tile * ROWS, ROWS)
            left = jnp.concatenate(
                [inverse[p, pl.ds(top, ROWS), pl.ds(pl.multiple_of(at, 256), 256)] for at in columns], axis=1
            )
            use(p, tile, jnp.dot(left, form[...], preferred_element_type=jnp.float32))


def first_kernel(inverse, own, right, left, across0, across1, *rest):
    out, form = rest[-2:]
    across = (across0, across1)
    _, x, z, _ = coordinates()

    def use(p, tile, value):
        out[p, pl.ds(pl.multiple_of(tile * ROWS, ROWS), ROWS), :] = value

    panels = [[own.at[p], right.at[p], left.at[p], across[p]] for p in range(2)]
    multiply(inverse, panels, form, columns_of(x, z >> 2), use)


def second_kernel(factors, inverse, before, own, right, left, across0, across1, *rest):
    keep, send, parts, form = rest[-4:]
    across = (across0, across1)
    y, x, z, core = coordinates()
    zl = z & 3

    def use(p, tile, value):
        w_re, w_im = factors[2 * p : 2 * p + 1, :], factors[2 * p + 1 : 2 * p + 2, :]
        total = before[p, pl.ds(pl.multiple_of(tile * ROWS, ROWS), ROWS), :] + value
        real, imag = total[:, :512], total[:, 512:]
        q_re = w_re * real - w_im * imag
        q_im = -(w_re * imag + w_im * real)
        for k in range(4):
            part = slice(k * 128, k * 128 + 128)
            for c in range(ROWS // 128):
                for side, q in enumerate((q_re, q_im)):
                    parts[k, tile * (ROWS // 128) + c, p, side] = q[c * 128 : c * 128 + 128, part]
            for pair in range(ROWS // 256):
                near = (tile * (ROWS // 256) + pair) ^ zl
                even = q_re[pair * 256 : pair * 256 + 128, part]
                odd = q_re[pair * 256 + 128 : pair * 256 + 256, part]
                kept = jnp.where(core == 0, even, odd)
                sent = jnp.where(core == 0, odd, even)
                if p == 0:
                    keep[k ^ y, near] = -kept
                    send[k ^ y, near] = -sent
                else:
                    keep[k ^ y, near] = keep[k ^ y, near] - kept
                    send[k ^ y, near] = send[k ^ y, near] - sent

    panels = [[own.at[p], right.at[p], left.at[p], across[p]] for p in range(2)]
    multiply(inverse, panels, form, columns_of(x, 1 - (z >> 2)), use)


def flip_kernel(panel, token0, token1, token2, token3, out):
    for p in range(2):
        for part in range(8):
            out[p, part] = panel[p, :, part * 128 : part * 128 + 128].T


def hop_kernel(far, from_left, from_right, right, left, to_right, to_left, relay_right, relay_left):
    _, _, z, _ = coordinates()
    zl = z & 3
    relay_right[...] = right[0]
    relay_left[...] = left[1]
    for edge, got, out in ((3, from_left, to_right), (0, from_right, to_left)):
        @pl.when(zl == edge)
        def _():
            for p in range(2):
                for part in range(8):
                    out[p, part] = far[p, :, part * 128 : part * 128 + 128].T

        @pl.when(zl != edge)
        def _():
            out[...] = got[...]


def gate_kernel(*refs):
    pass


def pair_kernel(keep, got, *rest):
    outs = rest[-4:]
    for bits in range(4):
        outs[bits][...] = keep[bits] + got[bits]


def add_kernel(a, b, *outs):
    y, _, _, _ = coordinates()
    total = a[...] + b[...]
    for target in range(4):
        for bits in range(4):
            @pl.when((y ^ bits) == target)
            def _():
                outs[bits][...] = total[target * 32 : target * 32 + 32]


def join_kernel(*refs):
    density, diag, outs = refs[:4], refs[4:8], refs[8:]
    small = (diag[0][...] + diag[1][...]) + (diag[2][...] + diag[3][...])
    for bits in range(4):
        outs[bits][:128] = (density[0][bits] + density[1][bits]) + (density[2][bits] + density[3][bits])
        outs[bits][128:] = small


def trace_kernel(factors, parts, diag, *rest):
    pieces, out, total = rest[:10], rest[10], rest[11]
    y, x, z, core = coordinates()
    zl = z & 3
    total[...] = jnp.zeros_like(total)
    rows_at = [
        zl,
        jnp.where(zl == 0, -1, zl - 1),
        jnp.where(zl == 3, -1, zl + 1),
        jnp.where(zl == 0, 3, jnp.where(zl == 1, -1, zl - 2)),
        jnp.where(zl == 3, 0, jnp.where(zl == 2, -1, zl + 2)),
    ]
    for index, piece in enumerate(pieces):
        row = rows_at[index % 5]
        c = row * 2 + (core if index < 5 else 1 - core)

        @pl.when(row >= 0)
        def _():
            for k in range(4):
                left = jnp.concatenate(
                    [piece[p, side * 4 + k] for p in range(2) for side in range(2)], axis=1
                )
                right = parts[k, c].reshape(512, 128)
                high = right.astype(jnp.bfloat16)
                low = (right - high.astype(jnp.float32)).astype(jnp.bfloat16)
                total[k] += jnp.dot(
                    left, jnp.concatenate([high, low], axis=1), preferred_element_type=jnp.float32
                )

    mine = jnp.zeros((8, 128), jnp.float32)
    for p in range(2):
        w_re, w_im = factors[2 * p : 2 * p + 1, :128], factors[2 * p + 1 : 2 * p + 2, :128]
        mine += w_re * diag[p, :, :128] - w_im * diag[p, :, 128:]
    row = pl.multiple_of((z * 2 + core) * 8, 8)
    total[x, pl.ds(row, 8), :128] = total[x, pl.ds(row, 8), :128] + mine
    for k in range(4):
        out[k ^ x] = (total[k, :, :128] + total[k, :, 128:]).T


def per_device(inverse_blocks, panel_blocks, ancestor_mask, diag_inverse, pole_weights, pole_order):
    y, xc, z, core = coordinates()
    zl = z & 3

    own = pl.pallas_call(
        mask_kernel,
        in_specs=[SMEM, VMEM],
        out_specs=VMEM,
        out_shape=jax.ShapeDtypeStruct((2, 128, 1024), jnp.bfloat16),
        cost_estimate=pl.CostEstimate(flops=0, bytes_accessed=MIB, transcendentals=0),
        compiler_params=pltpu.CompilerParams(vmem_limit_bytes=8 * MIB),
        name="mask",
    )(ancestor_mask, panel_blocks)
    factors = pl.pallas_call(
        factor_kernel,
        in_specs=[SMEM, VMEM, ANY],
        out_specs=VMEM,
        out_shape=jax.ShapeDtypeStruct((4, 512), jnp.float32),
        cost_estimate=pl.CostEstimate(flops=0, bytes_accessed=8192, transcendentals=0),
        compiler_params=pltpu.CompilerParams(vmem_limit_bytes=8 * MIB),
        name="factors",
    )(pole_order, pole_weights.T, own)
    far = z_partner(own, 4)
    right, left = along_x(own, 1), along_x(own, -1)
    relays = pl.pallas_call(
        relay_kernel,
        in_specs=[VMEM] * 2,
        out_specs=[VMEM] * 2,
        out_shape=[jax.ShapeDtypeStruct((128, 1024), jnp.bfloat16)] * 2,
        cost_estimate=pl.CostEstimate(flops=0, bytes_accessed=MIB, transcendentals=0),
        compiler_params=pltpu.CompilerParams(vmem_limit_bytes=8 * MIB),
        name="relay",
    )(right, left)
    near_panels = [own, right, left, along_x(relays[0], 1), along_x(relays[1], -1)]
    far_right, far_left = along_x(far, 1), along_x(far, -1)

    scratch = [pltpu.VMEM((1024, 1024), jnp.bfloat16)]
    inverse = pl.pallas_call(
        load_kernel,
        in_specs=[HBM, ANY],
        out_specs=VMEM,
        scratch_shapes=[pltpu.SemaphoreType.DMA((2, 2))],
        out_shape=jax.ShapeDtypeStruct((2, 1024, 2048), jnp.bfloat16),
        cost_estimate=pl.CostEstimate(flops=0, bytes_accessed=16 * MIB, transcendentals=0),
        compiler_params=pltpu.CompilerParams(vmem_limit_bytes=10 * MIB),
        name="load",
    )(inverse_blocks, factors)
    def flip(panel, *tokens):
        return pl.pallas_call(
            flip_kernel,
            in_specs=[VMEM] + [ANY] * 4,
            out_specs=VMEM,
            out_shape=jax.ShapeDtypeStruct((2, 8, 128, 128), jnp.bfloat16),
            cost_estimate=pl.CostEstimate(flops=0, bytes_accessed=MIB, transcendentals=0),
            compiler_params=pltpu.CompilerParams(vmem_limit_bytes=8 * MIB),
            name="flip",
        )(panel, *tokens)

    own_t = flip(own, far, *near_panels[3:], inverse)
    from_left, from_right = along_z(own_t, 1), along_z(own_t, -1)
    to_right, to_left, relay_right, relay_left = pl.pallas_call(
        hop_kernel,
        in_specs=[VMEM] * 5,
        out_specs=[VMEM] * 4,
        out_shape=[jax.ShapeDtypeStruct((2, 8, 128, 128), jnp.bfloat16)] * 2
        + [jax.ShapeDtypeStruct((128, 1024), jnp.bfloat16)] * 2,
        cost_estimate=pl.CostEstimate(flops=0, bytes_accessed=2 * MIB, transcendentals=0),
        compiler_params=pltpu.CompilerParams(vmem_limit_bytes=8 * MIB),
        name="hop",
    )(far, from_left, from_right, far_right, far_left)
    from_left2, from_right2 = along_z(to_right, 1), along_z(to_left, -1)
    far_panels = [far, far_right, far_left, along_x(relay_right, 1), along_x(relay_left, -1)]
    theirs = [other_core(piece) for piece in (own_t, from_left, from_right)]

    partial = pl.pallas_call(
        first_kernel,
        in_specs=[VMEM] * 6 + [ANY] * 3,
        out_specs=VMEM,
        scratch_shapes=scratch,
        out_shape=jax.ShapeDtypeStruct((2, 1024, 1024), jnp.float32),
        cost_estimate=pl.CostEstimate(flops=2 * 2 * 1024**3, bytes_accessed=4 * MIB, transcendentals=0),
        compiler_params=pltpu.CompilerParams(vmem_limit_bytes=NEAR_MIB * MIB),
        name="near",
    )(inverse, *near_panels, *theirs)

    keep, send, parts = pl.pallas_call(
        second_kernel,
        in_specs=[VMEM] * 8,
        out_specs=[VMEM] * 3,
        scratch_shapes=scratch,
        out_shape=[
            jax.ShapeDtypeStruct((4, 4, 128, 128), jnp.float32),
            jax.ShapeDtypeStruct((4, 4, 128, 128), jnp.float32),
            jax.ShapeDtypeStruct((4, 8, 2, 2, 128, 128), jnp.float32),
        ],
        cost_estimate=pl.CostEstimate(flops=0, bytes_accessed=0, transcendentals=0),
        compiler_params=pltpu.CompilerParams(vmem_limit_bytes=FAR_MIB * MIB),
        name="far",
    )(factors, inverse, partial, *far_panels)

    def gate(values, *tokens):
        return pl.pallas_call(
            gate_kernel,
            in_specs=[ANY] * (len(values) + len(tokens)),
            out_specs=[ANY] * len(values),
            out_shape=[jax.ShapeDtypeStruct(value.shape, value.dtype) for value in values],
            input_output_aliases={at: at for at in range(len(values))},
            cost_estimate=pl.CostEstimate(flops=0, bytes_accessed=0, transcendentals=0),
            compiler_params=pltpu.CompilerParams(vmem_limit_bytes=MIB),
            name="gate",
        )(*values, *tokens)

    from_left2, from_right2 = gate((from_left2, from_right2), keep)
    mine = [own_t, from_left, from_right, from_left2, from_right2]
    theirs = theirs + [other_core(piece) for piece in mine[3:]]
    (send,) = gate((send,), *theirs[3:])

    def small(body, name, shape, *operands):
        return pl.pallas_call(
            body,
            in_specs=([VMEM] * 2 + [ANY]) if len(operands) == 3 else [VMEM] * len(operands),
            out_specs=[VMEM] * 4,
            out_shape=[jax.ShapeDtypeStruct(shape, jnp.float32)] * 4,
            cost_estimate=pl.CostEstimate(flops=0, bytes_accessed=MIB, transcendentals=0),
            compiler_params=pltpu.CompilerParams(vmem_limit_bytes=8 * MIB),
            name=name,
        )(*operands)

    density = small(pair_kernel, "pair", (4, 128, 128), keep, other_core(send))
    traces = pl.pallas_call(
        trace_kernel,
        in_specs=[VMEM] * 13,
        out_specs=VMEM,
        scratch_shapes=[pltpu.VMEM((4, 128, 256), jnp.float32)],
        out_shape=jax.ShapeDtypeStruct((4, 128, 128), jnp.float32),
        cost_estimate=pl.CostEstimate(flops=2 * 4 * 128 * 256 * 4096, bytes_accessed=4 * MIB, transcendentals=0),
        compiler_params=pltpu.CompilerParams(vmem_limit_bytes=TRACE_MIB * MIB),
        name="trace",
    )(factors, parts, diag_inverse, *mine, *theirs)
    diag = small(pair_kernel, "cores", (128, 128), traces, other_core(traces), density[0])
    density = [density[0]] + [y_partner(density[bits], bits) for bits in (1, 2, 3)]
    diag = sum([x_partner(diag[bits], bits) for bits in (1, 2, 3)], diag[0])
    halves = [diag, z_mirror(diag)]
    diag = small(add_kernel, "nodes", (32, 128), *halves)
    diag = [diag[0]] + [y_partner(diag[bits], bits) for bits in (1, 2, 3)]
    joint = small(join_kernel, "join", (160, 128), *density, *diag)
    joint = sum([z_partner(joint[bits], bits) for bits in (1, 2, 3)], joint[0])
    diag = joint[128:]
    density = joint[:128] * lax.dynamic_index_in_dim(ancestor_mask[0], y, 0, keepdims=False).astype(jnp.float32)
    diag = lax.dynamic_slice_in_dim(diag, (z * 2 + core) * 8, 8, 1).T
    return density, diag


def solution(mesh):
    placed = (
        P("pole", "blk", None),
        P("pole", "blk", None),
        P("blk", None),
        P("pole", "blk", None),
        P(),
        P(),
    )
    return jax.shard_map(
        per_device,
        mesh=mesh,
        in_specs=placed,
        out_specs=(P("blk", "pole"), P("blk", "pole")),
        check_vma=False,
    )
```

```python
import jax
import jax.numpy as jnp
from jax import lax
from jax.experimental import pallas as pl
from jax.experimental.pallas import tpu as pltpu
from jax.sharding import PartitionSpec as P

X, Z, C, Y = 4, 8, 2, 4
ROWS = 512
VMEM = pl.BlockSpec(memory_space=pltpu.VMEM)
SMEM = pl.BlockSpec(memory_space=pltpu.SMEM)
ANY = pl.BlockSpec(memory_space=pl.ANY)
HBM = pl.BlockSpec(memory_space=pltpu.HBM)
MIB = 2**20
NEAR_MIB, FAR_MIB, TRACE_MIB = 8, 10, 8


def place(x, z, core):
    return (x % X) * Z * C + (z % Z) * C + core


PLACES = [(x, z, core) for x in range(X) for z in range(Z) for core in range(C)]


def along_x(value, by):
    return lax.ppermute(value, "blk", [(place(*at), place(at[0] + by, at[1], at[2])) for at in PLACES])


def along_z(value, by):
    return lax.ppermute(value, "blk", [(place(*at), place(at[0], at[1] + by, at[2])) for at in PLACES])


def x_partner(value, bits):
    return lax.ppermute(value, "blk", [(place(*at), place(at[0] ^ bits, at[1], at[2])) for at in PLACES])


def z_partner(value, bits):
    return lax.ppermute(value, "blk", [(place(*at), place(at[0], at[1] ^ bits, at[2])) for at in PLACES])


def z_mirror(value):
    return lax.ppermute(value, "blk", [(place(*at), place(at[0], 7 - at[1], at[2])) for at in PLACES])


def other_core(value):
    return lax.ppermute(value, "blk", [(place(*at), place(at[0], at[1], 1 - at[2])) for at in PLACES])


def y_partner(value, bits):
    return lax.ppermute(value, "pole", [(y, y ^ bits) for y in range(Y)])


def coordinates():
    rank = lax.axis_index("blk")
    return lax.axis_index("pole"), rank >> 4, (rank >> 1) & 7, rank & 1


def columns_of(x, side):
    return [(((x + by) & 3) * 2 + side) * 256 for by in (0, 3, 1, 2)]


def mask_kernel(mask, panel, own):
    for k in range(4):
        for t in range(2):
            part = slice(t * 512 + k * 128, t * 512 + k * 128 + 128)
            value = panel[:, :, part]
            own[:, :, part] = jnp.where(mask[0, k] != 0, value, jnp.zeros_like(value))


def factor_kernel(order, weights, token, factors):
    y, _, _, _ = coordinates()
    column = lax.broadcasted_iota(jnp.int32, (2, 8), 1)
    for p in range(2):
        chosen = jnp.where(column == order[y * 2 + p], weights[...], 0.0)
        factors[2 * p : 2 * p + 2, :] = jnp.broadcast_to(jnp.sum(chosen, axis=1, keepdims=True), (2, 512))


def build_form(form, panels):
    for step, panel_ref in enumerate(panels):
        top = step * 256
        form[top : top + 128, :] = panel_ref[...]
        form[top + 128 : top + 256, :512] = -panel_ref[:, 512:]
        form[top + 128 : top + 256, 512:] = panel_ref[:, :512]


def load_kernel(inverse, token, out, sems):
    copies = [
        pltpu.make_async_copy(
            inverse.at[p, pl.ds(half * 512, 512)], out.at[p, pl.ds(half * 512, 512)], sems.at[p, half]
        )
        for p in range(2)
        for half in range(2)
    ]
    for copy in copies:
        copy.start()
    for copy in copies:
        copy.wait()


def relay_kernel(right, left, relay_right, relay_left):
    relay_right[...] = right[0]
    relay_left[...] = left[1]


def multiply(inverse, panels, form, columns, use):
    for p in range(2):
        build_form(form, panels[p])

        @pl.loop(0, 1024 // ROWS)
        def _(tile):
            top = pl.multiple_of(tile * ROWS, ROWS)
            blocks = [inverse[p, pl.ds(top, ROWS), pl.ds(pl.multiple_of(at, 256), 256)] for at in columns]
            left = jnp.concatenate(blocks, axis=1) if len(blocks) > 1 else blocks[0]
            depth = 256 * len(columns)
            use(p, tile, jnp.dot(left, form[:depth, :], preferred_element_type=jnp.float32))


def first_kernel(inverse, own, right, left, across0, across1, out, form):
    across = (across0, across1)
    _, x, z, _ = coordinates()

    def use(p, tile, value):
        out[p, pl.ds(pl.multiple_of(tile * ROWS, ROWS), ROWS), :] = value

    panels = [[own.at[p], right.at[p], left.at[p], across[p]] for p in range(2)]
    multiply(inverse, panels, form, columns_of(x, z >> 2), use)


def middle_kernel(inverse, before, own, right, left, out, form):
    _, x, z, _ = coordinates()

    def use(p, tile, value):
        rows = pl.ds(pl.multiple_of(tile * ROWS, ROWS), ROWS)
        out[p, rows, :] = before[p, rows, :] + value

    panels = [[own.at[p], right.at[p], left.at[p]] for p in range(2)]
    multiply(inverse, panels, form, columns_of(x, 1 - (z >> 2))[:3], use)


def last_kernel(factors, inverse, before, across0, across1, keep, send, parts, form):
    y, x, z, core = coordinates()
    zl = z & 3

    def use(p, tile, value):
        w_re, w_im = factors[2 * p : 2 * p + 1, :], factors[2 * p + 1 : 2 * p + 2, :]
        total = before[p, pl.ds(pl.multiple_of(tile * ROWS, ROWS), ROWS), :] + value
        real, imag = total[:, :512], total[:, 512:]
        q_re = w_re * real - w_im * imag
        q_im = -(w_re * imag + w_im * real)
        for k in range(4):
            part = slice(k * 128, k * 128 + 128)
            for c in range(ROWS // 128):
                for side, q in enumerate((q_re, q_im)):
                    parts[k, tile * (ROWS // 128) + c, p, side] = q[c * 128 : c * 128 + 128, part]
            for pair in range(ROWS // 256):
                near = (tile * (ROWS // 256) + pair) ^ zl
                even = q_re[pair * 256 : pair * 256 + 128, part]
                odd = q_re[pair * 256 + 128 : pair * 256 + 256, part]
                kept = jnp.where(core == 0, even, odd)
                sent = jnp.where(core == 0, odd, even)
                if p == 0:
                    keep[k ^ y, near] = -kept
                    send[k ^ y, near] = -sent
                else:
                    keep[k ^ y, near] = keep[k ^ y, near] - kept
                    send[k ^ y, near] = send[k ^ y, near] - sent

    multiply(inverse, [[across0], [across1]], form, columns_of(x, 1 - (z >> 2))[3:], use)


def flip_kernel(panel, token0, token1, token2, token3, out):
    for p in range(2):
        for part in range(8):
            out[p, part] = panel[p, :, part * 128 : part * 128 + 128].T


def hop_kernel(far, from_left, from_right, right, left, *rest):
    to_right, to_left, relay_right, relay_left = rest[-4:]
    _, _, z, _ = coordinates()
    zl = z & 3
    relay_right[...] = right[0]
    relay_left[...] = left[1]
    for edge, got, out in ((3, from_left, to_right), (0, from_right, to_left)):
        @pl.when(zl == edge)
        def _():
            for p in range(2):
                for part in range(8):
                    out[p, part] = far[p, :, part * 128 : part * 128 + 128].T

        @pl.when(zl != edge)
        def _():
            out[...] = got[...]


def gate_kernel(*refs):
    pass


def pair_kernel(keep, got, *rest):
    outs = rest[-4:]
    for bits in range(4):
        outs[bits][...] = keep[bits] + got[bits]


def add_kernel(a, b, *outs):
    y, _, _, _ = coordinates()
    total = a[...] + b[...]
    for target in range(4):
        for bits in range(4):
            @pl.when((y ^ bits) == target)
            def _():
                outs[bits][...] = total[target * 32 : target * 32 + 32]


def join_kernel(*refs):
    density, diag, outs = refs[:4], refs[4:8], refs[8:]
    small = (diag[0][...] + diag[1][...]) + (diag[2][...] + diag[3][...])
    for bits in range(4):
        outs[bits][:128] = (density[0][bits] + density[1][bits]) + (density[2][bits] + density[3][bits])
        outs[bits][128:] = small


def trace_kernel(factors, parts, diag, *rest):
    pieces, out, total = rest[:10], rest[10], rest[11]
    y, x, z, core = coordinates()
    zl = z & 3
    total[...] = jnp.zeros_like(total)
    rows_at = [
        zl,
        jnp.where(zl == 0, -1, zl - 1),
        jnp.where(zl == 3, -1, zl + 1),
        jnp.where(zl == 0, 3, jnp.where(zl == 1, -1, zl - 2)),
        jnp.where(zl == 3, 0, jnp.where(zl == 2, -1, zl + 2)),
    ]
    for index, piece in enumerate(pieces):
        row = rows_at[index % 5]
        c = row * 2 + (core if index < 5 else 1 - core)

        @pl.when(row >= 0)
        def _():
            for k in range(4):
                left = jnp.concatenate(
                    [piece[p, side * 4 + k] for p in range(2) for side in range(2)], axis=1
                )
                right = parts[k, c].reshape(512, 128)
                high = right.astype(jnp.bfloat16)
                low = (right - high.astype(jnp.float32)).astype(jnp.bfloat16)
                total[k] += jnp.dot(
                    left, jnp.concatenate([high, low], axis=1), preferred_element_type=jnp.float32
                )

    mine = jnp.zeros((8, 128), jnp.float32)
    for p in range(2):
        w_re, w_im = factors[2 * p : 2 * p + 1, :128], factors[2 * p + 1 : 2 * p + 2, :128]
        mine += w_re * diag[p, :, :128] - w_im * diag[p, :, 128:]
    row = pl.multiple_of((z * 2 + core) * 8, 8)
    total[x, pl.ds(row, 8), :128] = total[x, pl.ds(row, 8), :128] + mine
    for k in range(4):
        out[k ^ x] = (total[k, :, :128] + total[k, :, 128:]).T


def finish_kernel(mask, a, b, c, d, density, diag, flipped):
    y, _, z, core = coordinates()
    total = (a[...] + b[...]) + (c[...] + d[...])
    density[...] = jnp.where(mask[0, y] != 0, total[:128], 0.0)
    flipped[...] = total[128:].T
    diag[...] = flipped[pl.ds(pl.multiple_of((z * 2 + core) * 8, 8), 8), :]


def per_device(inverse_blocks, panel_blocks, ancestor_mask, diag_inverse, pole_weights, pole_order):
    y, xc, z, core = coordinates()
    zl = z & 3

    own = pl.pallas_call(
        mask_kernel,
        in_specs=[SMEM, VMEM],
        out_specs=VMEM,
        out_shape=jax.ShapeDtypeStruct((2, 128, 1024), jnp.bfloat16),
        cost_estimate=pl.CostEstimate(flops=0, bytes_accessed=MIB, transcendentals=0),
        compiler_params=pltpu.CompilerParams(vmem_limit_bytes=8 * MIB),
        name="mask",
    )(ancestor_mask, panel_blocks)
    factors = pl.pallas_call(
        factor_kernel,
        in_specs=[SMEM, VMEM, ANY],
        out_specs=VMEM,
        out_shape=jax.ShapeDtypeStruct((4, 512), jnp.float32),
        cost_estimate=pl.CostEstimate(flops=0, bytes_accessed=8192, transcendentals=0),
        compiler_params=pltpu.CompilerParams(vmem_limit_bytes=8 * MIB),
        name="factors",
    )(pole_order, pole_weights.T, own)
    def gate(values, *tokens, weight=0):
        return pl.pallas_call(
            gate_kernel,
            in_specs=[ANY] * (len(values) + len(tokens)),
            out_specs=[ANY] * len(values),
            out_shape=[jax.ShapeDtypeStruct(value.shape, value.dtype) for value in values],
            input_output_aliases={at: at for at in range(len(values))},
            cost_estimate=pl.CostEstimate(flops=0, bytes_accessed=weight, transcendentals=0),
            compiler_params=pltpu.CompilerParams(vmem_limit_bytes=MIB),
            name="gate",
        )(*values, *tokens)

    (far,) = gate((z_partner(own, 4),), weight=0)
    right, left = along_x(own, 1), along_x(own, -1)
    relays = pl.pallas_call(
        relay_kernel,
        in_specs=[VMEM] * 2,
        out_specs=[VMEM] * 2,
        out_shape=[jax.ShapeDtypeStruct((128, 1024), jnp.bfloat16)] * 2,
        cost_estimate=pl.CostEstimate(flops=0, bytes_accessed=MIB, transcendentals=0),
        compiler_params=pltpu.CompilerParams(vmem_limit_bytes=8 * MIB),
        name="relay",
    )(right, left)
    near_panels = [own, right, left, along_x(relays[0], 1), along_x(relays[1], -1)]
    far_right, far_left = along_x(far, 1), along_x(far, -1)

    scratch = [pltpu.VMEM((1024, 1024), jnp.bfloat16)]
    inverse = pl.pallas_call(
        load_kernel,
        in_specs=[HBM, ANY],
        out_specs=VMEM,
        scratch_shapes=[pltpu.SemaphoreType.DMA((2, 2))],
        out_shape=jax.ShapeDtypeStruct((2, 1024, 2048), jnp.bfloat16),
        cost_estimate=pl.CostEstimate(flops=0, bytes_accessed=16 * MIB, transcendentals=0),
        compiler_params=pltpu.CompilerParams(vmem_limit_bytes=10 * MIB),
        name="load",
    )(inverse_blocks, factors)
    def flip(panel, *tokens):
        return pl.pallas_call(
            flip_kernel,
            in_specs=[VMEM] + [ANY] * 4,
            out_specs=VMEM,
            out_shape=jax.ShapeDtypeStruct((2, 8, 128, 128), jnp.bfloat16),
            cost_estimate=pl.CostEstimate(flops=0, bytes_accessed=MIB, transcendentals=0),
            compiler_params=pltpu.CompilerParams(vmem_limit_bytes=8 * MIB),
            name="flip",
        )(panel, *tokens)

    own_t = flip(own, far, *near_panels[3:], inverse)
    partial = pl.pallas_call(
        first_kernel,
        in_specs=[VMEM] * 6,
        out_specs=VMEM,
        scratch_shapes=scratch,
        out_shape=jax.ShapeDtypeStruct((2, 1024, 1024), jnp.float32),
        cost_estimate=pl.CostEstimate(flops=2 * 2 * 1024**3, bytes_accessed=4 * MIB, transcendentals=0),
        compiler_params=pltpu.CompilerParams(vmem_limit_bytes=NEAR_MIB * MIB),
        name="near",
    )(inverse, *near_panels)

    from_left, from_right = along_z(own_t, 1), along_z(own_t, -1)
    from_left, from_right = gate((from_left, from_right), partial)
    theirs = [other_core(piece) for piece in (own_t, from_left, from_right)]
    to_right, to_left, relay_right, relay_left = pl.pallas_call(
        hop_kernel,
        in_specs=[VMEM] * 5 + [ANY] * 4,
        out_specs=[VMEM] * 4,
        out_shape=[jax.ShapeDtypeStruct((2, 8, 128, 128), jnp.bfloat16)] * 2
        + [jax.ShapeDtypeStruct((128, 1024), jnp.bfloat16)] * 2,
        cost_estimate=pl.CostEstimate(flops=0, bytes_accessed=2 * MIB, transcendentals=0),
        compiler_params=pltpu.CompilerParams(vmem_limit_bytes=8 * MIB),
        name="hop",
    )(far, from_left, from_right, far_right, far_left, partial, *theirs)
    from_left2, from_right2 = along_z(to_right, 1), along_z(to_left, -1)
    far_panels = [far, far_right, far_left, along_x(relay_right, 1), along_x(relay_left, -1)]

    partial = pl.pallas_call(
        middle_kernel,
        in_specs=[VMEM] * 5,
        out_specs=VMEM,
        scratch_shapes=scratch,
        out_shape=jax.ShapeDtypeStruct((2, 1024, 1024), jnp.float32),
        input_output_aliases={1: 0},
        cost_estimate=pl.CostEstimate(flops=3 * 1024**3, bytes_accessed=4 * MIB, transcendentals=0),
        compiler_params=pltpu.CompilerParams(vmem_limit_bytes=NEAR_MIB * MIB),
        name="middle",
    )(inverse, partial, *far_panels[:3])

    keep, send, parts = pl.pallas_call(
        last_kernel,
        in_specs=[VMEM] * 5,
        out_specs=[VMEM] * 3,
        scratch_shapes=scratch,
        out_shape=[
            jax.ShapeDtypeStruct((4, 4, 128, 128), jnp.float32),
            jax.ShapeDtypeStruct((4, 4, 128, 128), jnp.float32),
            jax.ShapeDtypeStruct((4, 8, 2, 2, 128, 128), jnp.float32),
        ],
        cost_estimate=pl.CostEstimate(flops=0, bytes_accessed=0, transcendentals=0),
        compiler_params=pltpu.CompilerParams(vmem_limit_bytes=FAR_MIB * MIB),
        name="last",
    )(factors, inverse, partial, *far_panels[3:])

    from_left2, from_right2 = gate((from_left2, from_right2), keep)
    mine = [own_t, from_left, from_right, from_left2, from_right2]
    theirs = theirs + [other_core(piece) for piece in mine[3:]]
    (send,) = gate((send,), *theirs[3:])

    def small(body, name, shape, *operands):
        return pl.pallas_call(
            body,
            in_specs=([VMEM] * 2 + [ANY]) if len(operands) == 3 else [VMEM] * len(operands),
            out_specs=[VMEM] * 4,
            out_shape=[jax.ShapeDtypeStruct(shape, jnp.float32)] * 4,
            cost_estimate=pl.CostEstimate(flops=0, bytes_accessed=MIB, transcendentals=0),
            compiler_params=pltpu.CompilerParams(vmem_limit_bytes=8 * MIB),
            name=name,
        )(*operands)

    density = small(pair_kernel, "pair", (4, 128, 128), keep, other_core(send))
    traces = pl.pallas_call(
        trace_kernel,
        in_specs=[VMEM] * 13,
        out_specs=VMEM,
        scratch_shapes=[pltpu.VMEM((4, 128, 256), jnp.float32)],
        out_shape=jax.ShapeDtypeStruct((4, 128, 128), jnp.float32),
        cost_estimate=pl.CostEstimate(flops=2 * 4 * 128 * 256 * 4096, bytes_accessed=4 * MIB, transcendentals=0),
        compiler_params=pltpu.CompilerParams(vmem_limit_bytes=TRACE_MIB * MIB),
        name="trace",
    )(factors, parts, diag_inverse, *mine, *theirs)
    diag = small(pair_kernel, "cores", (128, 128), traces, other_core(traces), density[0])
    density = [density[0]] + [y_partner(density[bits], bits) for bits in (1, 2, 3)]
    diag = sum([x_partner(diag[bits], bits) for bits in (1, 2, 3)], diag[0])
    halves = [diag, z_mirror(diag)]
    diag = small(add_kernel, "nodes", (32, 128), *halves)
    diag = [diag[0]] + [y_partner(diag[bits], bits) for bits in (1, 2, 3)]
    joint = small(join_kernel, "join", (160, 128), *density, *diag)
    joint = [joint[0]] + [z_partner(joint[bits], bits) for bits in (1, 2, 3)]
    density, diag = pl.pallas_call(
        finish_kernel,
        in_specs=[SMEM] + [VMEM] * 4,
        out_specs=[VMEM] * 2,
        scratch_shapes=[pltpu.VMEM((128, 32), jnp.float32)],
        out_shape=[
            jax.ShapeDtypeStruct((128, 128), jnp.float32),
            jax.ShapeDtypeStruct((8, 32), jnp.float32),
        ],
        cost_estimate=pl.CostEstimate(flops=0, bytes_accessed=MIB, transcendentals=0),
        compiler_params=pltpu.CompilerParams(vmem_limit_bytes=8 * MIB),
        name="finish",
    )(ancestor_mask, *joint)
    return density, diag


def solution(mesh):
    placed = (
        P("pole", "blk", None),
        P("pole", "blk", None),
        P("blk", None),
        P("pole", "blk", None),
        P(),
        P(),
    )
    return jax.shard_map(
        per_device,
        mesh=mesh,
        in_specs=placed,
        out_specs=(P("blk", "pole"), P("blk", "pole")),
        check_vma=False,
    )
```

```python
import jax
import jax.numpy as jnp
from jax import lax
from jax.experimental import pallas as pl
from jax.experimental.pallas import tpu as pltpu
from jax.sharding import PartitionSpec as P

X, Z, C, Y = 4, 8, 2, 4
ROWS = 512
VMEM = pl.BlockSpec(memory_space=pltpu.VMEM)
SMEM = pl.BlockSpec(memory_space=pltpu.SMEM)
ANY = pl.BlockSpec(memory_space=pl.ANY)
HBM = pl.BlockSpec(memory_space=pltpu.HBM)
MIB = 2**20
NEAR_MIB, FAR_MIB, TRACE_MIB = 8, 10, 8


def place(x, z, core):
    return (x % X) * Z * C + (z % Z) * C + core


PLACES = [(x, z, core) for x in range(X) for z in range(Z) for core in range(C)]


def along_x(value, by):
    return lax.ppermute(value, "blk", [(place(*at), place(at[0] + by, at[1], at[2])) for at in PLACES])


def along_z(value, by):
    return lax.ppermute(value, "blk", [(place(*at), place(at[0], at[1] + by, at[2])) for at in PLACES])


def x_partner(value, bits):
    return lax.ppermute(value, "blk", [(place(*at), place(at[0] ^ bits, at[1], at[2])) for at in PLACES])


def z_partner(value, bits):
    return lax.ppermute(value, "blk", [(place(*at), place(at[0], at[1] ^ bits, at[2])) for at in PLACES])


def z_mirror(value):
    return lax.ppermute(value, "blk", [(place(*at), place(at[0], 7 - at[1], at[2])) for at in PLACES])


def other_core(value):
    return lax.ppermute(value, "blk", [(place(*at), place(at[0], at[1], 1 - at[2])) for at in PLACES])


def y_partner(value, bits):
    return lax.ppermute(value, "pole", [(y, y ^ bits) for y in range(Y)])


def coordinates():
    rank = lax.axis_index("blk")
    return lax.axis_index("pole"), rank >> 4, (rank >> 1) & 7, rank & 1


def columns_of(x, side):
    return [(((x + by) & 3) * 2 + side) * 256 for by in (0, 3, 1, 2)]


def mask_kernel(mask, panel, own):
    for k in range(4):
        for t in range(2):
            part = slice(t * 512 + k * 128, t * 512 + k * 128 + 128)
            value = panel[:, :, part]
            own[:, :, part] = jnp.where(mask[0, k] != 0, value, jnp.zeros_like(value))


def factor_kernel(order, weights, token, factors):
    y, _, _, _ = coordinates()
    column = lax.broadcasted_iota(jnp.int32, (2, 8), 1)
    for p in range(2):
        chosen = jnp.where(column == order[y * 2 + p], weights[...], 0.0)
        factors[2 * p : 2 * p + 2, :] = jnp.broadcast_to(jnp.sum(chosen, axis=1, keepdims=True), (2, 512))


def build_form(form, panels):
    for step, panel_ref in enumerate(panels):
        top = step * 256
        form[top : top + 128, :] = panel_ref[...]
        form[top + 128 : top + 256, :512] = -panel_ref[:, 512:]
        form[top + 128 : top + 256, 512:] = panel_ref[:, :512]


def load_kernel(inverse, token, out, sems):
    copies = [
        pltpu.make_async_copy(
            inverse.at[p, pl.ds(half * 512, 512)], out.at[p, pl.ds(half * 512, 512)], sems.at[p, half]
        )
        for p in range(2)
        for half in range(2)
    ]
    for copy in copies:
        copy.start()
    for copy in copies:
        copy.wait()


def relay_kernel(right, left, token, relay_right, relay_left):
    relay_right[...] = right[0]
    relay_left[...] = left[1]


def multiply(inverse, panels, form, columns, use):
    for p in range(2):
        build_form(form, panels[p])

        @pl.loop(0, 1024 // ROWS)
        def _(tile):
            top = pl.multiple_of(tile * ROWS, ROWS)
            blocks = [inverse[p, pl.ds(top, ROWS), pl.ds(pl.multiple_of(at, 256), 256)] for at in columns]
            left = jnp.concatenate(blocks, axis=1) if len(blocks) > 1 else blocks[0]
            depth = 256 * len(columns)
            use(p, tile, jnp.dot(left, form[:depth, :], preferred_element_type=jnp.float32))


def first_kernel(inverse, own, right, left, across0, across1, out, form):
    across = (across0, across1)
    _, x, z, _ = coordinates()

    def use(p, tile, value):
        out[p, pl.ds(pl.multiple_of(tile * ROWS, ROWS), ROWS), :] = value

    panels = [[own.at[p], right.at[p], left.at[p], across[p]] for p in range(2)]
    multiply(inverse, panels, form, columns_of(x, z >> 2), use)


def middle_kernel(inverse, before, own, right, left, *rest):
    out, form = rest[-2:]
    _, x, z, _ = coordinates()

    def use(p, tile, value):
        rows = pl.ds(pl.multiple_of(tile * ROWS, ROWS), ROWS)
        out[p, rows, :] = before[p, rows, :] + value

    panels = [[own.at[p], right.at[p], left.at[p]] for p in range(2)]
    multiply(inverse, panels, form, columns_of(x, 1 - (z >> 2))[:3], use)


def last_kernel(factors, inverse, before, across0, across1, keep, send, parts, form):
    y, x, z, core = coordinates()
    zl = z & 3

    def use(p, tile, value):
        w_re, w_im = factors[2 * p : 2 * p + 1, :], factors[2 * p + 1 : 2 * p + 2, :]
        total = before[p, pl.ds(pl.multiple_of(tile * ROWS, ROWS), ROWS), :] + value
        real, imag = total[:, :512], total[:, 512:]
        q_re = w_re * real - w_im * imag
        q_im = -(w_re * imag + w_im * real)
        for k in range(4):
            part = slice(k * 128, k * 128 + 128)
            for c in range(ROWS // 128):
                for side, q in enumerate((q_re, q_im)):
                    parts[k, tile * (ROWS // 128) + c, p, side] = q[c * 128 : c * 128 + 128, part]
            for pair in range(ROWS // 256):
                near = (tile * (ROWS // 256) + pair) ^ zl
                even = q_re[pair * 256 : pair * 256 + 128, part]
                odd = q_re[pair * 256 + 128 : pair * 256 + 256, part]
                kept = jnp.where(core == 0, even, odd)
                sent = jnp.where(core == 0, odd, even)
                if p == 0:
                    keep[k ^ y, near] = -kept
                    send[k ^ y, near] = -sent
                else:
                    keep[k ^ y, near] = keep[k ^ y, near] - kept
                    send[k ^ y, near] = send[k ^ y, near] - sent

    multiply(inverse, [[across0], [across1]], form, columns_of(x, 1 - (z >> 2))[3:], use)


def flip_kernel(panel, token0, token1, token2, token3, out):
    for p in range(2):
        for part in range(8):
            out[p, part] = panel[p, :, part * 128 : part * 128 + 128].T


def hop_kernel(far, from_left, from_right, token, to_right, to_left):
    _, _, z, _ = coordinates()
    zl = z & 3
    for edge, got, out in ((3, from_left, to_right), (0, from_right, to_left)):
        @pl.when(zl == edge)
        def _():
            for p in range(2):
                for part in range(8):
                    out[p, part] = far[p, :, part * 128 : part * 128 + 128].T

        @pl.when(zl != edge)
        def _():
            out[...] = got[...]


def gate_kernel(*refs):
    pass


def pair_kernel(keep, got, *rest):
    outs = rest[-4:]
    for bits in range(4):
        outs[bits][...] = keep[bits] + got[bits]


def add_kernel(a, b, *outs):
    y, _, _, _ = coordinates()
    total = a[...] + b[...]
    for target in range(4):
        for bits in range(4):
            @pl.when((y ^ bits) == target)
            def _():
                outs[bits][...] = total[target * 32 : target * 32 + 32]


def join_kernel(*refs):
    density, diag, outs = refs[:4], refs[4:8], refs[8:]
    small = (diag[0][...] + diag[1][...]) + (diag[2][...] + diag[3][...])
    for bits in range(4):
        outs[bits][:128] = (density[0][bits] + density[1][bits]) + (density[2][bits] + density[3][bits])
        outs[bits][128:] = small


def trace_kernel(factors, parts, diag, *rest):
    pieces, out, total = rest[:10], rest[10], rest[11]
    y, x, z, core = coordinates()
    zl = z & 3
    total[...] = jnp.zeros_like(total)
    rows_at = [
        zl,
        jnp.where(zl == 0, -1, zl - 1),
        jnp.where(zl == 3, -1, zl + 1),
        jnp.where(zl == 0, 3, jnp.where(zl == 1, -1, zl - 2)),
        jnp.where(zl == 3, 0, jnp.where(zl == 2, -1, zl + 2)),
    ]
    for index, piece in enumerate(pieces):
        row = rows_at[index % 5]
        c = row * 2 + (core if index < 5 else 1 - core)

        @pl.when(row >= 0)
        def _():
            for k in range(4):
                left = jnp.concatenate(
                    [piece[p, side * 4 + k] for p in range(2) for side in range(2)], axis=1
                )
                right = parts[k, c].reshape(512, 128)
                high = right.astype(jnp.bfloat16)
                low = (right - high.astype(jnp.float32)).astype(jnp.bfloat16)
                total[k] += jnp.dot(
                    left, jnp.concatenate([high, low], axis=1), preferred_element_type=jnp.float32
                )

    mine = jnp.zeros((8, 128), jnp.float32)
    for p in range(2):
        w_re, w_im = factors[2 * p : 2 * p + 1, :128], factors[2 * p + 1 : 2 * p + 2, :128]
        mine += w_re * diag[p, :, :128] - w_im * diag[p, :, 128:]
    row = pl.multiple_of((z * 2 + core) * 8, 8)
    total[x, pl.ds(row, 8), :128] = total[x, pl.ds(row, 8), :128] + mine
    for k in range(4):
        out[k ^ x] = (total[k, :, :128] + total[k, :, 128:]).T


def finish_kernel(mask, a, b, c, d, density, diag, flipped):
    y, _, z, core = coordinates()
    total = (a[...] + b[...]) + (c[...] + d[...])
    density[...] = jnp.where(mask[0, y] != 0, total[:128], 0.0)
    flipped[...] = total[128:].T
    diag[...] = flipped[pl.ds(pl.multiple_of((z * 2 + core) * 8, 8), 8), :]


def per_device(inverse_blocks, panel_blocks, ancestor_mask, diag_inverse, pole_weights, pole_order):
    y, xc, z, core = coordinates()
    zl = z & 3

    own = pl.pallas_call(
        mask_kernel,
        in_specs=[SMEM, VMEM],
        out_specs=VMEM,
        out_shape=jax.ShapeDtypeStruct((2, 128, 1024), jnp.bfloat16),
        cost_estimate=pl.CostEstimate(flops=0, bytes_accessed=MIB, transcendentals=0),
        compiler_params=pltpu.CompilerParams(vmem_limit_bytes=8 * MIB),
        name="mask",
    )(ancestor_mask, panel_blocks)
    factors = pl.pallas_call(
        factor_kernel,
        in_specs=[SMEM, VMEM, ANY],
        out_specs=VMEM,
        out_shape=jax.ShapeDtypeStruct((4, 512), jnp.float32),
        cost_estimate=pl.CostEstimate(flops=0, bytes_accessed=8192, transcendentals=0),
        compiler_params=pltpu.CompilerParams(vmem_limit_bytes=8 * MIB),
        name="factors",
    )(pole_order, pole_weights.T, own)
    def gate(values, *tokens, weight=0):
        return pl.pallas_call(
            gate_kernel,
            in_specs=[ANY] * (len(values) + len(tokens)),
            out_specs=[ANY] * len(values),
            out_shape=[jax.ShapeDtypeStruct(value.shape, value.dtype) for value in values],
            input_output_aliases={at: at for at in range(len(values))},
            cost_estimate=pl.CostEstimate(flops=0, bytes_accessed=weight, transcendentals=0),
            compiler_params=pltpu.CompilerParams(vmem_limit_bytes=MIB),
            name="gate",
        )(*values, *tokens)

    (far,) = gate((z_partner(own, 4),), weight=0)
    right, left = along_x(own, 1), along_x(own, -1)
    def relay(right, left, token):
        halves = pl.pallas_call(
            relay_kernel,
            in_specs=[VMEM] * 2 + [ANY],
            out_specs=[VMEM] * 2,
            out_shape=[jax.ShapeDtypeStruct((128, 1024), jnp.bfloat16)] * 2,
            cost_estimate=pl.CostEstimate(flops=0, bytes_accessed=MIB, transcendentals=0),
            compiler_params=pltpu.CompilerParams(vmem_limit_bytes=8 * MIB),
            name="relay",
        )(right, left, token)
        return halves

    halves = relay(right, left, own)
    near_panels = [own, right, left, along_x(halves[0], 1), along_x(halves[1], -1)]
    far_right, far_left = along_x(far, 1), along_x(far, -1)

    scratch = [pltpu.VMEM((1024, 1024), jnp.bfloat16)]
    inverse = pl.pallas_call(
        load_kernel,
        in_specs=[HBM, ANY],
        out_specs=VMEM,
        scratch_shapes=[pltpu.SemaphoreType.DMA((2, 2))],
        out_shape=jax.ShapeDtypeStruct((2, 1024, 2048), jnp.bfloat16),
        cost_estimate=pl.CostEstimate(flops=0, bytes_accessed=16 * MIB, transcendentals=0),
        compiler_params=pltpu.CompilerParams(vmem_limit_bytes=10 * MIB),
        name="load",
    )(inverse_blocks, factors)
    def flip(panel, *tokens):
        return pl.pallas_call(
            flip_kernel,
            in_specs=[VMEM] + [ANY] * 4,
            out_specs=VMEM,
            out_shape=jax.ShapeDtypeStruct((2, 8, 128, 128), jnp.bfloat16),
            cost_estimate=pl.CostEstimate(flops=0, bytes_accessed=MIB, transcendentals=0),
            compiler_params=pltpu.CompilerParams(vmem_limit_bytes=8 * MIB),
            name="flip",
        )(panel, *tokens)

    own_t = flip(own, far, *near_panels[3:], inverse)
    partial = pl.pallas_call(
        first_kernel,
        in_specs=[VMEM] * 6,
        out_specs=VMEM,
        scratch_shapes=scratch,
        out_shape=jax.ShapeDtypeStruct((2, 1024, 1024), jnp.float32),
        cost_estimate=pl.CostEstimate(flops=2 * 2 * 1024**3, bytes_accessed=4 * MIB, transcendentals=0),
        compiler_params=pltpu.CompilerParams(vmem_limit_bytes=NEAR_MIB * MIB),
        name="near",
    )(inverse, *near_panels)

    from_left, from_right = along_z(own_t, 1), along_z(own_t, -1)
    from_left, from_right = gate((from_left, from_right), partial)
    to_right, to_left = pl.pallas_call(
        hop_kernel,
        in_specs=[VMEM] * 3 + [ANY],
        out_specs=[VMEM] * 2,
        out_shape=[jax.ShapeDtypeStruct((2, 8, 128, 128), jnp.bfloat16)] * 2,
        cost_estimate=pl.CostEstimate(flops=0, bytes_accessed=2 * MIB, transcendentals=0),
        compiler_params=pltpu.CompilerParams(vmem_limit_bytes=8 * MIB),
        name="hop",
    )(far, from_left, from_right, partial)
    from_left2, from_right2 = along_z(to_right, 1), along_z(to_left, -1)
    halves = relay(far_right, far_left, to_right)
    far_panels = [far, far_right, far_left, along_x(halves[0], 1), along_x(halves[1], -1)]
    theirs = [other_core(piece) for piece in (own_t, from_left, from_right)]

    partial = pl.pallas_call(
        middle_kernel,
        in_specs=[VMEM] * 5 + [ANY] * 3,
        out_specs=VMEM,
        scratch_shapes=scratch,
        out_shape=jax.ShapeDtypeStruct((2, 1024, 1024), jnp.float32),
        input_output_aliases={1: 0},
        cost_estimate=pl.CostEstimate(flops=3 * 1024**3, bytes_accessed=4 * MIB, transcendentals=0),
        compiler_params=pltpu.CompilerParams(vmem_limit_bytes=NEAR_MIB * MIB),
        name="middle",
    )(inverse, partial, *far_panels[:3], *theirs)

    keep, send, parts = pl.pallas_call(
        last_kernel,
        in_specs=[VMEM] * 5,
        out_specs=[VMEM] * 3,
        scratch_shapes=scratch,
        out_shape=[
            jax.ShapeDtypeStruct((4, 4, 128, 128), jnp.float32),
            jax.ShapeDtypeStruct((4, 4, 128, 128), jnp.float32),
            jax.ShapeDtypeStruct((4, 8, 2, 2, 128, 128), jnp.float32),
        ],
        cost_estimate=pl.CostEstimate(flops=0, bytes_accessed=0, transcendentals=0),
        compiler_params=pltpu.CompilerParams(vmem_limit_bytes=FAR_MIB * MIB),
        name="last",
    )(factors, inverse, partial, *far_panels[3:])

    from_left2, from_right2 = gate((from_left2, from_right2), keep)
    mine = [own_t, from_left, from_right, from_left2, from_right2]
    theirs = theirs + [other_core(piece) for piece in mine[3:]]
    (send,) = gate((send,), *theirs[3:])

    def small(body, name, shape, *operands):
        return pl.pallas_call(
            body,
            in_specs=([VMEM] * 2 + [ANY]) if len(operands) == 3 else [VMEM] * len(operands),
            out_specs=[VMEM] * 4,
            out_shape=[jax.ShapeDtypeStruct(shape, jnp.float32)] * 4,
            cost_estimate=pl.CostEstimate(flops=0, bytes_accessed=MIB, transcendentals=0),
            compiler_params=pltpu.CompilerParams(vmem_limit_bytes=8 * MIB),
            name=name,
        )(*operands)

    density = small(pair_kernel, "pair", (4, 128, 128), keep, other_core(send))
    traces = pl.pallas_call(
        trace_kernel,
        in_specs=[VMEM] * 13,
        out_specs=VMEM,
        scratch_shapes=[pltpu.VMEM((4, 128, 256), jnp.float32)],
        out_shape=jax.ShapeDtypeStruct((4, 128, 128), jnp.float32),
        cost_estimate=pl.CostEstimate(flops=2 * 4 * 128 * 256 * 4096, bytes_accessed=4 * MIB, transcendentals=0),
        compiler_params=pltpu.CompilerParams(vmem_limit_bytes=TRACE_MIB * MIB),
        name="trace",
    )(factors, parts, diag_inverse, *mine, *theirs)
    diag = small(pair_kernel, "cores", (128, 128), traces, other_core(traces), density[0])
    density = [density[0]] + [y_partner(density[bits], bits) for bits in (1, 2, 3)]
    diag = sum([x_partner(diag[bits], bits) for bits in (1, 2, 3)], diag[0])
    halves = [diag, z_mirror(diag)]
    diag = small(add_kernel, "nodes", (32, 128), *halves)
    diag = [diag[0]] + [y_partner(diag[bits], bits) for bits in (1, 2, 3)]
    joint = small(join_kernel, "join", (160, 128), *density, *diag)
    joint = [joint[0]] + [z_partner(joint[bits], bits) for bits in (1, 2, 3)]
    density, diag = pl.pallas_call(
        finish_kernel,
        in_specs=[SMEM] + [VMEM] * 4,
        out_specs=[VMEM] * 2,
        scratch_shapes=[pltpu.VMEM((128, 32), jnp.float32)],
        out_shape=[
            jax.ShapeDtypeStruct((128, 128), jnp.float32),
            jax.ShapeDtypeStruct((8, 32), jnp.float32),
        ],
        cost_estimate=pl.CostEstimate(flops=0, bytes_accessed=MIB, transcendentals=0),
        compiler_params=pltpu.CompilerParams(vmem_limit_bytes=8 * MIB),
        name="finish",
    )(ancestor_mask, *joint)
    return density, diag


def solution(mesh):
    placed = (
        P("pole", "blk", None),
        P("pole", "blk", None),
        P("blk", None),
        P("pole", "blk", None),
        P(),
        P(),
    )
    return jax.shard_map(
        per_device,
        mesh=mesh,
        in_specs=placed,
        out_specs=(P("blk", "pole"), P("blk", "pole")),
        check_vma=False,
    )
```

```python
import jax
import jax.numpy as jnp
from jax import lax
from jax.experimental import pallas as pl
from jax.experimental.pallas import tpu as pltpu
from jax.sharding import PartitionSpec as P

X, Z, C, Y = 4, 8, 2, 4
ROWS = 512
VMEM = pl.BlockSpec(memory_space=pltpu.VMEM)
SMEM = pl.BlockSpec(memory_space=pltpu.SMEM)
ANY = pl.BlockSpec(memory_space=pl.ANY)
HBM = pl.BlockSpec(memory_space=pltpu.HBM)
MIB = 2**20
NEAR_MIB, FAR_MIB, TRACE_MIB = 8, 10, 8


def place(x, z, core):
    return (x % X) * Z * C + (z % Z) * C + core


PLACES = [(x, z, core) for x in range(X) for z in range(Z) for core in range(C)]


def along_x(value, by):
    return lax.ppermute(value, "blk", [(place(*at), place(at[0] + by, at[1], at[2])) for at in PLACES])


def along_z(value, by):
    return lax.ppermute(value, "blk", [(place(*at), place(at[0], at[1] + by, at[2])) for at in PLACES])


def x_partner(value, bits):
    return lax.ppermute(value, "blk", [(place(*at), place(at[0] ^ bits, at[1], at[2])) for at in PLACES])


def z_partner(value, bits):
    return lax.ppermute(value, "blk", [(place(*at), place(at[0], at[1] ^ bits, at[2])) for at in PLACES])


def z_mirror(value):
    return lax.ppermute(value, "blk", [(place(*at), place(at[0], 7 - at[1], at[2])) for at in PLACES])


def other_core(value):
    return lax.ppermute(value, "blk", [(place(*at), place(at[0], at[1], 1 - at[2])) for at in PLACES])


def y_partner(value, bits):
    return lax.ppermute(value, "pole", [(y, y ^ bits) for y in range(Y)])


def coordinates():
    rank = lax.axis_index("blk")
    return lax.axis_index("pole"), rank >> 4, (rank >> 1) & 7, rank & 1


def columns_of(x, side):
    return [(((x + by) & 3) * 2 + side) * 256 for by in (0, 3, 1, 2)]


def mask_kernel(mask, panel, own):
    for k in range(4):
        for t in range(2):
            part = slice(t * 512 + k * 128, t * 512 + k * 128 + 128)
            value = panel[:, :, part]
            own[:, :, part] = jnp.where(mask[0, k] != 0, value, jnp.zeros_like(value))


def factor_kernel(order, weights, token, factors):
    y, _, _, _ = coordinates()
    column = lax.broadcasted_iota(jnp.int32, (2, 8), 1)
    for p in range(2):
        chosen = jnp.where(column == order[y * 2 + p], weights[...], 0.0)
        factors[2 * p : 2 * p + 2, :] = jnp.broadcast_to(jnp.sum(chosen, axis=1, keepdims=True), (2, 512))


def build_form(form, panels):
    for step, panel_ref in enumerate(panels):
        top = step * 256
        form[top : top + 128, :] = panel_ref[...]
        form[top + 128 : top + 256, :512] = -panel_ref[:, 512:]
        form[top + 128 : top + 256, 512:] = panel_ref[:, :512]


def load_kernel(inverse, token, out, sems):
    copies = [
        pltpu.make_async_copy(
            inverse.at[p, pl.ds(half * 512, 512)], out.at[p, pl.ds(half * 512, 512)], sems.at[p, half]
        )
        for p in range(2)
        for half in range(2)
    ]
    for copy in copies:
        copy.start()
    for copy in copies:
        copy.wait()


def relay_kernel(right, left, token, relay_right, relay_left):
    relay_right[...] = right[0]
    relay_left[...] = left[1]


def multiply(inverse, panels, form, columns, use):
    for p in range(2):
        build_form(form, panels[p])

        @pl.loop(0, 1024 // ROWS)
        def _(tile):
            top = pl.multiple_of(tile * ROWS, ROWS)
            blocks = [inverse[p, pl.ds(top, ROWS), pl.ds(pl.multiple_of(at, 256), 256)] for at in columns]
            left = jnp.concatenate(blocks, axis=1) if len(blocks) > 1 else blocks[0]
            depth = 256 * len(columns)
            use(p, tile, jnp.dot(left, form[:depth, :], preferred_element_type=jnp.float32))


def first_kernel(inverse, own, right, left, across0, across1, out, form):
    across = (across0, across1)
    _, x, z, _ = coordinates()

    def use(p, tile, value):
        out[p, pl.ds(pl.multiple_of(tile * ROWS, ROWS), ROWS), :] = value

    panels = [[own.at[p], right.at[p], left.at[p], across[p]] for p in range(2)]
    multiply(inverse, panels, form, columns_of(x, z >> 2), use)


def middle_kernel(inverse, before, own, right, left, *rest):
    out, form = rest[-2:]
    _, x, z, _ = coordinates()

    def use(p, tile, value):
        rows = pl.ds(pl.multiple_of(tile * ROWS, ROWS), ROWS)
        out[p, rows, :] = before[p, rows, :] + value

    panels = [[own.at[p], right.at[p], left.at[p]] for p in range(2)]
    multiply(inverse, panels, form, columns_of(x, 1 - (z >> 2))[:3], use)


def last_kernel(factors, inverse, before, across0, across1, keep, send, parts, form):
    y, x, z, core = coordinates()
    zl = z & 3

    def use(p, tile, value):
        w_re, w_im = factors[2 * p : 2 * p + 1, :], factors[2 * p + 1 : 2 * p + 2, :]
        total = before[p, pl.ds(pl.multiple_of(tile * ROWS, ROWS), ROWS), :] + value
        real, imag = total[:, :512], total[:, 512:]
        q_re = w_re * real - w_im * imag
        q_im = -(w_re * imag + w_im * real)
        for k in range(4):
            part = slice(k * 128, k * 128 + 128)
            for c in range(ROWS // 128):
                for side, q in enumerate((q_re, q_im)):
                    parts[k, tile * (ROWS // 128) + c, p, side] = q[c * 128 : c * 128 + 128, part]
            for pair in range(ROWS // 256):
                near = (tile * (ROWS // 256) + pair) ^ zl
                even = q_re[pair * 256 : pair * 256 + 128, part]
                odd = q_re[pair * 256 + 128 : pair * 256 + 256, part]
                kept = jnp.where(core == 0, even, odd)
                sent = jnp.where(core == 0, odd, even)
                if p == 0:
                    keep[k ^ y, near] = -kept
                    send[k ^ y, near] = -sent
                else:
                    keep[k ^ y, near] = keep[k ^ y, near] - kept
                    send[k ^ y, near] = send[k ^ y, near] - sent

    multiply(inverse, [[across0], [across1]], form, columns_of(x, 1 - (z >> 2))[3:], use)


def flip_kernel(panel, token0, token1, token2, token3, out):
    for p in range(2):
        for part in range(8):
            out[p, part] = panel[p, :, part * 128 : part * 128 + 128].T


def hop_kernel(far, from_left, from_right, token, to_right, to_left):
    _, _, z, _ = coordinates()
    zl = z & 3
    for edge, got, out in ((3, from_left, to_right), (0, from_right, to_left)):
        @pl.when(zl == edge)
        def _():
            for p in range(2):
                for part in range(8):
                    out[p, part] = far[p, :, part * 128 : part * 128 + 128].T

        @pl.when(zl != edge)
        def _():
            out[...] = got[...]


def gate_kernel(*refs):
    pass


def pair_kernel(keep, got, *rest):
    outs = rest[-4:]
    for bits in range(4):
        outs[bits][...] = keep[bits] + got[bits]


def add_kernel(a, b, *outs):
    y, _, _, _ = coordinates()
    total = (a[...] + b[...]).T
    for target in range(4):
        for bits in range(4):
            @pl.when((y ^ bits) == target)
            def _():
                outs[bits][:, :64] = total[target * 32 : target * 32 + 32]
                outs[bits][:, 64:] = jnp.zeros((32, 64), jnp.float32)


def join_kernel(*refs):
    density, diag, outs = refs[:4], refs[4:8], refs[8:]
    small = (diag[0][...] + diag[1][...]) + (diag[2][...] + diag[3][...])
    for bits in range(4):
        outs[bits][:128] = (density[0][bits] + density[1][bits]) + (density[2][bits] + density[3][bits])
        outs[bits][128:] = small


def trace_kernel(factors, parts, diag, *rest):
    pieces, keep, send, total = rest[:10], rest[10], rest[11], rest[12]
    y, x, z, core = coordinates()
    zl = z & 3
    total[...] = jnp.zeros_like(total)
    rows_at = [
        zl,
        jnp.where(zl == 0, -1, zl - 1),
        jnp.where(zl == 3, -1, zl + 1),
        jnp.where(zl == 0, 3, jnp.where(zl == 1, -1, zl - 2)),
        jnp.where(zl == 3, 0, jnp.where(zl == 2, -1, zl + 2)),
    ]
    for index, piece in enumerate(pieces):
        row = rows_at[index % 5]
        c = row * 2 + (core if index < 5 else 1 - core)

        @pl.when(row >= 0)
        def _():
            for k in range(4):
                left = jnp.concatenate(
                    [piece[p, side * 4 + k] for p in range(2) for side in range(2)], axis=1
                )
                right = parts[k, c].reshape(512, 128)
                high = right.astype(jnp.bfloat16)
                low = (right - high.astype(jnp.float32)).astype(jnp.bfloat16)
                total[k] += jnp.dot(
                    left, jnp.concatenate([high, low], axis=1), preferred_element_type=jnp.float32
                )

    mine = jnp.zeros((8, 128), jnp.float32)
    for p in range(2):
        w_re, w_im = factors[2 * p : 2 * p + 1, :128], factors[2 * p + 1 : 2 * p + 2, :128]
        mine += w_re * diag[p, :, :128] - w_im * diag[p, :, 128:]
    row = pl.multiple_of((z * 2 + core) * 8, 8)
    total[x, pl.ds(row, 8), :128] = total[x, pl.ds(row, 8), :128] + mine
    for k in range(4):
        value = (total[k, :, :128] + total[k, :, 128:]).reshape(8, 2, 8, 128)
        keep[k ^ x] = jnp.where(core == 0, value[:, 0], value[:, 1]).reshape(64, 128)
        send[k ^ x] = jnp.where(core == 0, value[:, 1], value[:, 0]).reshape(64, 128)


def finish_kernel(mask, a, b, c, d, density, diag, flipped):
    y, _, z, _ = coordinates()
    total = (a[...] + b[...]) + (c[...] + d[...])
    density[...] = jnp.where(mask[0, y] != 0, total[:128], 0.0)
    flipped[...] = total[128:].T
    diag[...] = flipped[pl.ds(pl.multiple_of(z * 8, 8), 8), :]


def per_device(inverse_blocks, panel_blocks, ancestor_mask, diag_inverse, pole_weights, pole_order):
    y, xc, z, core = coordinates()
    zl = z & 3

    own = pl.pallas_call(
        mask_kernel,
        in_specs=[SMEM, VMEM],
        out_specs=VMEM,
        out_shape=jax.ShapeDtypeStruct((2, 128, 1024), jnp.bfloat16),
        cost_estimate=pl.CostEstimate(flops=0, bytes_accessed=MIB, transcendentals=0),
        compiler_params=pltpu.CompilerParams(vmem_limit_bytes=8 * MIB),
        name="mask",
    )(ancestor_mask, panel_blocks)
    factors = pl.pallas_call(
        factor_kernel,
        in_specs=[SMEM, VMEM, ANY],
        out_specs=VMEM,
        out_shape=jax.ShapeDtypeStruct((4, 512), jnp.float32),
        cost_estimate=pl.CostEstimate(flops=0, bytes_accessed=8192, transcendentals=0),
        compiler_params=pltpu.CompilerParams(vmem_limit_bytes=8 * MIB),
        name="factors",
    )(pole_order, pole_weights.T, own)
    def gate(values, *tokens, weight=0):
        return pl.pallas_call(
            gate_kernel,
            in_specs=[ANY] * (len(values) + len(tokens)),
            out_specs=[ANY] * len(values),
            out_shape=[jax.ShapeDtypeStruct(value.shape, value.dtype) for value in values],
            input_output_aliases={at: at for at in range(len(values))},
            cost_estimate=pl.CostEstimate(flops=0, bytes_accessed=weight, transcendentals=0),
            compiler_params=pltpu.CompilerParams(vmem_limit_bytes=MIB),
            name="gate",
        )(*values, *tokens)

    (far,) = gate((z_partner(own, 4),), weight=0)
    right, left = along_x(own, 1), along_x(own, -1)
    def relay(right, left, token):
        halves = pl.pallas_call(
            relay_kernel,
            in_specs=[VMEM] * 2 + [ANY],
            out_specs=[VMEM] * 2,
            out_shape=[jax.ShapeDtypeStruct((128, 1024), jnp.bfloat16)] * 2,
            cost_estimate=pl.CostEstimate(flops=0, bytes_accessed=MIB, transcendentals=0),
            compiler_params=pltpu.CompilerParams(vmem_limit_bytes=8 * MIB),
            name="relay",
        )(right, left, token)
        return halves

    halves = relay(right, left, own)
    near_panels = [own, right, left, along_x(halves[0], 1), along_x(halves[1], -1)]
    far_right, far_left = along_x(far, 1), along_x(far, -1)

    scratch = [pltpu.VMEM((1024, 1024), jnp.bfloat16)]
    inverse = pl.pallas_call(
        load_kernel,
        in_specs=[HBM, ANY],
        out_specs=VMEM,
        scratch_shapes=[pltpu.SemaphoreType.DMA((2, 2))],
        out_shape=jax.ShapeDtypeStruct((2, 1024, 2048), jnp.bfloat16),
        cost_estimate=pl.CostEstimate(flops=0, bytes_accessed=16 * MIB, transcendentals=0),
        compiler_params=pltpu.CompilerParams(vmem_limit_bytes=10 * MIB),
        name="load",
    )(inverse_blocks, factors)
    def flip(panel, *tokens):
        return pl.pallas_call(
            flip_kernel,
            in_specs=[VMEM] + [ANY] * 4,
            out_specs=VMEM,
            out_shape=jax.ShapeDtypeStruct((2, 8, 128, 128), jnp.bfloat16),
            cost_estimate=pl.CostEstimate(flops=0, bytes_accessed=MIB, transcendentals=0),
            compiler_params=pltpu.CompilerParams(vmem_limit_bytes=8 * MIB),
            name="flip",
        )(panel, *tokens)

    own_t = flip(own, far, *near_panels[3:], inverse)
    partial = pl.pallas_call(
        first_kernel,
        in_specs=[VMEM] * 6,
        out_specs=VMEM,
        scratch_shapes=scratch,
        out_shape=jax.ShapeDtypeStruct((2, 1024, 1024), jnp.float32),
        cost_estimate=pl.CostEstimate(flops=2 * 2 * 1024**3, bytes_accessed=4 * MIB, transcendentals=0),
        compiler_params=pltpu.CompilerParams(vmem_limit_bytes=NEAR_MIB * MIB),
        name="near",
    )(inverse, *near_panels)

    from_left, from_right = along_z(own_t, 1), along_z(own_t, -1)
    from_left, from_right = gate((from_left, from_right), partial)
    to_right, to_left = pl.pallas_call(
        hop_kernel,
        in_specs=[VMEM] * 3 + [ANY],
        out_specs=[VMEM] * 2,
        out_shape=[jax.ShapeDtypeStruct((2, 8, 128, 128), jnp.bfloat16)] * 2,
        cost_estimate=pl.CostEstimate(flops=0, bytes_accessed=2 * MIB, transcendentals=0),
        compiler_params=pltpu.CompilerParams(vmem_limit_bytes=8 * MIB),
        name="hop",
    )(far, from_left, from_right, partial)
    from_left2, from_right2 = along_z(to_right, 1), along_z(to_left, -1)
    halves = relay(far_right, far_left, to_right)
    far_panels = [far, far_right, far_left, along_x(halves[0], 1), along_x(halves[1], -1)]
    theirs = [other_core(piece) for piece in (own_t, from_left, from_right)]

    partial = pl.pallas_call(
        middle_kernel,
        in_specs=[VMEM] * 5 + [ANY] * 3,
        out_specs=VMEM,
        scratch_shapes=scratch,
        out_shape=jax.ShapeDtypeStruct((2, 1024, 1024), jnp.float32),
        input_output_aliases={1: 0},
        cost_estimate=pl.CostEstimate(flops=3 * 1024**3, bytes_accessed=4 * MIB, transcendentals=0),
        compiler_params=pltpu.CompilerParams(vmem_limit_bytes=NEAR_MIB * MIB),
        name="middle",
    )(inverse, partial, *far_panels[:3], *theirs)

    keep, send, parts = pl.pallas_call(
        last_kernel,
        in_specs=[VMEM] * 5,
        out_specs=[VMEM] * 3,
        scratch_shapes=scratch,
        out_shape=[
            jax.ShapeDtypeStruct((4, 4, 128, 128), jnp.float32),
            jax.ShapeDtypeStruct((4, 4, 128, 128), jnp.float32),
            jax.ShapeDtypeStruct((4, 8, 2, 2, 128, 128), jnp.float32),
        ],
        cost_estimate=pl.CostEstimate(flops=0, bytes_accessed=0, transcendentals=0),
        compiler_params=pltpu.CompilerParams(vmem_limit_bytes=FAR_MIB * MIB),
        name="last",
    )(factors, inverse, partial, *far_panels[3:])

    from_left2, from_right2 = gate((from_left2, from_right2), keep)
    mine = [own_t, from_left, from_right, from_left2, from_right2]
    theirs = theirs + [other_core(piece) for piece in mine[3:]]
    (send,) = gate((send,), *theirs[3:])

    def small(body, name, shape, *operands):
        return pl.pallas_call(
            body,
            in_specs=([VMEM] * 2 + [ANY]) if len(operands) == 3 else [VMEM] * len(operands),
            out_specs=[VMEM] * 4,
            out_shape=[jax.ShapeDtypeStruct(shape, jnp.float32)] * 4,
            cost_estimate=pl.CostEstimate(flops=0, bytes_accessed=MIB, transcendentals=0),
            compiler_params=pltpu.CompilerParams(vmem_limit_bytes=8 * MIB),
            name=name,
        )(*operands)

    density = small(pair_kernel, "pair", (4, 128, 128), keep, other_core(send))
    t_keep, t_send = pl.pallas_call(
        trace_kernel,
        in_specs=[VMEM] * 13,
        out_specs=[VMEM] * 2,
        scratch_shapes=[pltpu.VMEM((4, 128, 256), jnp.float32)],
        out_shape=[jax.ShapeDtypeStruct((4, 64, 128), jnp.float32)] * 2,
        cost_estimate=pl.CostEstimate(flops=2 * 4 * 128 * 256 * 4096, bytes_accessed=4 * MIB, transcendentals=0),
        compiler_params=pltpu.CompilerParams(vmem_limit_bytes=TRACE_MIB * MIB),
        name="trace",
    )(factors, parts, diag_inverse, *mine, *theirs)
    diag = small(pair_kernel, "cores", (64, 128), t_keep, other_core(t_send), density[0])
    density = [density[0]] + [y_partner(density[bits], bits) for bits in (1, 2, 3)]
    diag = sum([x_partner(diag[bits], bits) for bits in (1, 2, 3)], diag[0])
    halves = [diag, z_mirror(diag)]
    diag = small(add_kernel, "nodes", (32, 128), *halves)
    diag = [diag[0]] + [y_partner(diag[bits], bits) for bits in (1, 2, 3)]
    joint = small(join_kernel, "join", (160, 128), *density, *diag)
    joint = [joint[0]] + [z_partner(joint[bits], bits) for bits in (1, 2, 3)]
    density, diag = pl.pallas_call(
        finish_kernel,
        in_specs=[SMEM] + [VMEM] * 4,
        out_specs=[VMEM] * 2,
        scratch_shapes=[pltpu.VMEM((128, 32), jnp.float32)],
        out_shape=[
            jax.ShapeDtypeStruct((128, 128), jnp.float32),
            jax.ShapeDtypeStruct((8, 32), jnp.float32),
        ],
        cost_estimate=pl.CostEstimate(flops=0, bytes_accessed=MIB, transcendentals=0),
        compiler_params=pltpu.CompilerParams(vmem_limit_bytes=8 * MIB),
        name="finish",
    )(ancestor_mask, *joint)
    return density, diag


def solution(mesh):
    placed = (
        P("pole", "blk", None),
        P("pole", "blk", None),
        P("blk", None),
        P("pole", "blk", None),
        P(),
        P(),
    )
    return jax.shard_map(
        per_device,
        mesh=mesh,
        in_specs=placed,
        out_specs=(P("blk", "pole"), P("blk", "pole")),
        check_vma=False,
    )
```

```python
import jax
import jax.numpy as jnp
from jax import lax
from jax.experimental import pallas as pl
from jax.experimental.pallas import tpu as pltpu
from jax.sharding import PartitionSpec as P

X, Z, C, Y = 4, 8, 2, 4
ROWS = 512
VMEM = pl.BlockSpec(memory_space=pltpu.VMEM)
SMEM = pl.BlockSpec(memory_space=pltpu.SMEM)
ANY = pl.BlockSpec(memory_space=pl.ANY)
HBM = pl.BlockSpec(memory_space=pltpu.HBM)
MIB = 2**20
NEAR_MIB, FAR_MIB, TRACE_MIB = 8, 10, 8


def place(x, z, core):
    return (x % X) * Z * C + (z % Z) * C + core


PLACES = [(x, z, core) for x in range(X) for z in range(Z) for core in range(C)]


def along_x(value, by):
    return lax.ppermute(value, "blk", [(place(*at), place(at[0] + by, at[1], at[2])) for at in PLACES])


def along_z(value, by):
    return lax.ppermute(value, "blk", [(place(*at), place(at[0], at[1] + by, at[2])) for at in PLACES])


def x_partner(value, bits):
    return lax.ppermute(value, "blk", [(place(*at), place(at[0] ^ bits, at[1], at[2])) for at in PLACES])


def z_partner(value, bits):
    return lax.ppermute(value, "blk", [(place(*at), place(at[0], at[1] ^ bits, at[2])) for at in PLACES])


def other_core(value):
    return lax.ppermute(value, "blk", [(place(*at), place(at[0], at[1], 1 - at[2])) for at in PLACES])


def y_partner(value, bits):
    return lax.ppermute(value, "pole", [(y, y ^ bits) for y in range(Y)])


def coordinates():
    rank = lax.axis_index("blk")
    return lax.axis_index("pole"), rank >> 4, (rank >> 1) & 7, rank & 1


def columns_of(x, side):
    return [(((x + by) & 3) * 2 + side) * 256 for by in (0, 3, 1, 2)]


def mask_kernel(mask, panel, own):
    for k in range(4):
        for t in range(2):
            part = slice(t * 512 + k * 128, t * 512 + k * 128 + 128)
            value = panel[:, :, part]
            own[:, :, part] = jnp.where(mask[0, k] != 0, value, jnp.zeros_like(value))


def factor_kernel(order, weights, token, factors):
    y, _, _, _ = coordinates()
    column = lax.broadcasted_iota(jnp.int32, (2, 8), 1)
    for p in range(2):
        chosen = jnp.where(column == order[y * 2 + p], weights[...], 0.0)
        factors[2 * p : 2 * p + 2, :] = jnp.broadcast_to(jnp.sum(chosen, axis=1, keepdims=True), (2, 512))


def build_form(form, panels):
    for step, panel_ref in enumerate(panels):
        top = step * 256
        form[top : top + 128, :] = panel_ref[...]
        form[top + 128 : top + 256, :512] = -panel_ref[:, 512:]
        form[top + 128 : top + 256, 512:] = panel_ref[:, :512]


def load_kernel(inverse, token, out, sems):
    copies = [
        pltpu.make_async_copy(
            inverse.at[p, pl.ds(half * 512, 512)], out.at[p, pl.ds(half * 512, 512)], sems.at[p, half]
        )
        for p in range(2)
        for half in range(2)
    ]
    for copy in copies:
        copy.start()
    for copy in copies:
        copy.wait()


def relay_kernel(right, left, token, relay_right, relay_left):
    relay_right[...] = right[0]
    relay_left[...] = left[1]


def multiply(inverse, panels, form, columns, use):
    for p in range(2):
        build_form(form, panels[p])

        @pl.loop(0, 1024 // ROWS)
        def _(tile):
            top = pl.multiple_of(tile * ROWS, ROWS)
            blocks = [inverse[p, pl.ds(top, ROWS), pl.ds(pl.multiple_of(at, 256), 256)] for at in columns]
            left = jnp.concatenate(blocks, axis=1) if len(blocks) > 1 else blocks[0]
            depth = 256 * len(columns)
            use(p, tile, jnp.dot(left, form[:depth, :], preferred_element_type=jnp.float32))


def first_kernel(inverse, own, right, left, across0, across1, out, form):
    across = (across0, across1)
    _, x, z, _ = coordinates()

    def use(p, tile, value):
        out[p, pl.ds(pl.multiple_of(tile * ROWS, ROWS), ROWS), :] = value

    panels = [[own.at[p], right.at[p], left.at[p], across[p]] for p in range(2)]
    multiply(inverse, panels, form, columns_of(x, z >> 2), use)


def middle_kernel(inverse, before, own, right, left, *rest):
    out, form = rest[-2:]
    _, x, z, _ = coordinates()

    def use(p, tile, value):
        rows = pl.ds(pl.multiple_of(tile * ROWS, ROWS), ROWS)
        out[p, rows, :] = before[p, rows, :] + value

    panels = [[own.at[p], right.at[p], left.at[p]] for p in range(2)]
    multiply(inverse, panels, form, columns_of(x, 1 - (z >> 2))[:3], use)


def last_kernel(factors, inverse, before, across0, across1, keep, send, parts, form):
    y, x, z, core = coordinates()
    zl = z & 3

    def use(p, tile, value):
        w_re, w_im = factors[2 * p : 2 * p + 1, :], factors[2 * p + 1 : 2 * p + 2, :]
        total = before[p, pl.ds(pl.multiple_of(tile * ROWS, ROWS), ROWS), :] + value
        real, imag = total[:, :512], total[:, 512:]
        q_re = w_re * real - w_im * imag
        q_im = -(w_re * imag + w_im * real)
        for k in range(4):
            part = slice(k * 128, k * 128 + 128)
            for c in range(ROWS // 128):
                for side, q in enumerate((q_re, q_im)):
                    parts[k, tile * (ROWS // 128) + c, p, side] = q[c * 128 : c * 128 + 128, part]
            for pair in range(ROWS // 256):
                near = (tile * (ROWS // 256) + pair) ^ zl
                even = q_re[pair * 256 : pair * 256 + 128, part]
                odd = q_re[pair * 256 + 128 : pair * 256 + 256, part]
                kept = jnp.where(core == 0, even, odd)
                sent = jnp.where(core == 0, odd, even)
                if p == 0:
                    keep[k ^ y, near] = -kept
                    send[k ^ y, near] = -sent
                else:
                    keep[k ^ y, near] = keep[k ^ y, near] - kept
                    send[k ^ y, near] = send[k ^ y, near] - sent

    multiply(inverse, [[across0], [across1]], form, columns_of(x, 1 - (z >> 2))[3:], use)


def flip_kernel(panel, token0, token1, token2, token3, out):
    for p in range(2):
        for part in range(8):
            out[p, part] = panel[p, :, part * 128 : part * 128 + 128].T


def hop_kernel(far, from_left, from_right, token, to_right, to_left):
    _, _, z, _ = coordinates()
    zl = z & 3
    for edge, got, out in ((3, from_left, to_right), (0, from_right, to_left)):
        @pl.when(zl == edge)
        def _():
            for p in range(2):
                for part in range(8):
                    out[p, part] = far[p, :, part * 128 : part * 128 + 128].T

        @pl.when(zl != edge)
        def _():
            out[...] = got[...]


def gate_kernel(*refs):
    pass


def pair_kernel(keep, got, *rest):
    outs = rest[-4:]
    for bits in range(4):
        outs[bits][...] = keep[bits] + got[bits]


def add_kernel(a, b, *outs):
    y, _, _, _ = coordinates()
    total = (a[...] + b[...]).T
    for target in range(4):
        for bits in range(4):
            @pl.when((y ^ bits) == target)
            def _():
                outs[bits][:, :64] = total[target * 32 : target * 32 + 32]
                outs[bits][:, 64:] = jnp.zeros((32, 64), jnp.float32)


def join_kernel(*refs):
    density, diag, outs = refs[:4], refs[4:8], refs[8:]
    small = (diag[0][...] + diag[1][...]) + (diag[2][...] + diag[3][...])
    for bits in range(4):
        outs[bits][:128] = (density[0][bits] + density[1][bits]) + (density[2][bits] + density[3][bits])
        outs[bits][128:] = small


def piece_rows(zl):
    return [
        zl,
        jnp.where(zl == 0, -1, zl - 1),
        jnp.where(zl == 3, -1, zl + 1),
        jnp.where(zl == 0, 3, jnp.where(zl == 1, -1, zl - 2)),
        jnp.where(zl == 3, 0, jnp.where(zl == 2, -1, zl + 2)),
    ]


def add_pieces(parts, pieces, rows, side, total):
    for piece, row in zip(pieces, rows):
        @pl.when(row >= 0)
        def _():
            for k in range(4):
                left = jnp.concatenate(
                    [piece[p, part * 4 + k] for p in range(2) for part in range(2)], axis=1
                )
                right = parts[k, row * 2 + side].reshape(512, 128)
                high = right.astype(jnp.bfloat16)
                low = (right - high.astype(jnp.float32)).astype(jnp.bfloat16)
                total[k] += jnp.dot(
                    left, jnp.concatenate([high, low], axis=1), preferred_element_type=jnp.float32
                )


def trace_kernel(factors, parts, diag, *rest):
    mine, theirs, total = rest[:3], rest[3:6], rest[6]
    _, x, z, core = coordinates()
    rows = piece_rows(z & 3)
    total[...] = jnp.zeros_like(total)
    add_pieces(parts, mine, rows[:3], core, total)
    add_pieces(parts, theirs, rows[:3], 1 - core, total)
    own = jnp.zeros((8, 128), jnp.float32)
    for p in range(2):
        w_re, w_im = factors[2 * p : 2 * p + 1, :128], factors[2 * p + 1 : 2 * p + 2, :128]
        own += w_re * diag[p, :, :128] - w_im * diag[p, :, 128:]
    at = pl.multiple_of((z * 2 + core) * 8, 8)
    total[x, pl.ds(at, 8), :128] = total[x, pl.ds(at, 8), :128] + own


def rest_kernel(parts, before, mine0, mine1, theirs0, theirs1, keep, send, total):
    _, x, z, core = coordinates()
    total[...] = before[...]
    rows = piece_rows(z & 3)[3:]
    add_pieces(parts, (mine0, mine1), rows, core, total)
    add_pieces(parts, (theirs0, theirs1), rows, 1 - core, total)
    for k in range(4):
        value = (total[k, :, :128] + total[k, :, 128:]).reshape(8, 2, 8, 128)
        keep[k ^ x] = jnp.where(core == 0, value[:, 0], value[:, 1]).reshape(64, 128)
        send[k ^ x] = jnp.where(core == 0, value[:, 1], value[:, 0]).reshape(64, 128)


def finish_kernel(mask, a, b, c, d, density, diag, flipped):
    y, _, z, _ = coordinates()
    total = (a[...] + b[...]) + (c[...] + d[...])
    density[...] = jnp.where(mask[0, y] != 0, total[:128], 0.0)
    flipped[...] = total[128:].T
    diag[...] = flipped[pl.ds(pl.multiple_of(z * 8, 8), 8), :]


def per_device(inverse_blocks, panel_blocks, ancestor_mask, diag_inverse, pole_weights, pole_order):
    y, xc, z, core = coordinates()
    zl = z & 3

    own = pl.pallas_call(
        mask_kernel,
        in_specs=[SMEM, VMEM],
        out_specs=VMEM,
        out_shape=jax.ShapeDtypeStruct((2, 128, 1024), jnp.bfloat16),
        cost_estimate=pl.CostEstimate(flops=0, bytes_accessed=MIB, transcendentals=0),
        compiler_params=pltpu.CompilerParams(vmem_limit_bytes=8 * MIB),
        name="mask",
    )(ancestor_mask, panel_blocks)
    factors = pl.pallas_call(
        factor_kernel,
        in_specs=[SMEM, VMEM, ANY],
        out_specs=VMEM,
        out_shape=jax.ShapeDtypeStruct((4, 512), jnp.float32),
        cost_estimate=pl.CostEstimate(flops=0, bytes_accessed=8192, transcendentals=0),
        compiler_params=pltpu.CompilerParams(vmem_limit_bytes=8 * MIB),
        name="factors",
    )(pole_order, pole_weights.T, own)
    def gate(values, *tokens, weight=0):
        return pl.pallas_call(
            gate_kernel,
            in_specs=[ANY] * (len(values) + len(tokens)),
            out_specs=[ANY] * len(values),
            out_shape=[jax.ShapeDtypeStruct(value.shape, value.dtype) for value in values],
            input_output_aliases={at: at for at in range(len(values))},
            cost_estimate=pl.CostEstimate(flops=0, bytes_accessed=weight, transcendentals=0),
            compiler_params=pltpu.CompilerParams(vmem_limit_bytes=MIB),
            name="gate",
        )(*values, *tokens)

    (far,) = gate((z_partner(own, 4),), weight=0)
    right, left = along_x(own, 1), along_x(own, -1)
    def relay(right, left, token):
        halves = pl.pallas_call(
            relay_kernel,
            in_specs=[VMEM] * 2 + [ANY],
            out_specs=[VMEM] * 2,
            out_shape=[jax.ShapeDtypeStruct((128, 1024), jnp.bfloat16)] * 2,
            cost_estimate=pl.CostEstimate(flops=0, bytes_accessed=MIB, transcendentals=0),
            compiler_params=pltpu.CompilerParams(vmem_limit_bytes=8 * MIB),
            name="relay",
        )(right, left, token)
        return halves

    halves = relay(right, left, own)
    near_panels = [own, right, left, along_x(halves[0], 1), along_x(halves[1], -1)]
    far_right, far_left = along_x(far, 1), along_x(far, -1)

    scratch = [pltpu.VMEM((1024, 1024), jnp.bfloat16)]
    inverse = pl.pallas_call(
        load_kernel,
        in_specs=[HBM, ANY],
        out_specs=VMEM,
        scratch_shapes=[pltpu.SemaphoreType.DMA((2, 2))],
        out_shape=jax.ShapeDtypeStruct((2, 1024, 2048), jnp.bfloat16),
        cost_estimate=pl.CostEstimate(flops=0, bytes_accessed=16 * MIB, transcendentals=0),
        compiler_params=pltpu.CompilerParams(vmem_limit_bytes=10 * MIB),
        name="load",
    )(inverse_blocks, factors)
    def flip(panel, *tokens):
        return pl.pallas_call(
            flip_kernel,
            in_specs=[VMEM] + [ANY] * 4,
            out_specs=VMEM,
            out_shape=jax.ShapeDtypeStruct((2, 8, 128, 128), jnp.bfloat16),
            cost_estimate=pl.CostEstimate(flops=0, bytes_accessed=MIB, transcendentals=0),
            compiler_params=pltpu.CompilerParams(vmem_limit_bytes=8 * MIB),
            name="flip",
        )(panel, *tokens)

    own_t = flip(own, far, *near_panels[3:], inverse)
    partial = pl.pallas_call(
        first_kernel,
        in_specs=[VMEM] * 6,
        out_specs=VMEM,
        scratch_shapes=scratch,
        out_shape=jax.ShapeDtypeStruct((2, 1024, 1024), jnp.float32),
        cost_estimate=pl.CostEstimate(flops=2 * 2 * 1024**3, bytes_accessed=4 * MIB, transcendentals=0),
        compiler_params=pltpu.CompilerParams(vmem_limit_bytes=NEAR_MIB * MIB),
        name="near",
    )(inverse, *near_panels)

    from_left, from_right = along_z(own_t, 1), along_z(own_t, -1)
    from_left, from_right = gate((from_left, from_right), partial)
    to_right, to_left = pl.pallas_call(
        hop_kernel,
        in_specs=[VMEM] * 3 + [ANY],
        out_specs=[VMEM] * 2,
        out_shape=[jax.ShapeDtypeStruct((2, 8, 128, 128), jnp.bfloat16)] * 2,
        cost_estimate=pl.CostEstimate(flops=0, bytes_accessed=2 * MIB, transcendentals=0),
        compiler_params=pltpu.CompilerParams(vmem_limit_bytes=8 * MIB),
        name="hop",
    )(far, from_left, from_right, partial)
    from_left2, from_right2 = along_z(to_right, 1), along_z(to_left, -1)
    halves = relay(far_right, far_left, to_right)
    far_panels = [far, far_right, far_left, along_x(halves[0], 1), along_x(halves[1], -1)]
    theirs = [other_core(piece) for piece in (own_t, from_left, from_right)]

    partial = pl.pallas_call(
        middle_kernel,
        in_specs=[VMEM] * 5 + [ANY] * 3,
        out_specs=VMEM,
        scratch_shapes=scratch,
        out_shape=jax.ShapeDtypeStruct((2, 1024, 1024), jnp.float32),
        input_output_aliases={1: 0},
        cost_estimate=pl.CostEstimate(flops=3 * 1024**3, bytes_accessed=4 * MIB, transcendentals=0),
        compiler_params=pltpu.CompilerParams(vmem_limit_bytes=NEAR_MIB * MIB),
        name="middle",
    )(inverse, partial, *far_panels[:3], *theirs)

    keep, send, parts = pl.pallas_call(
        last_kernel,
        in_specs=[VMEM] * 5,
        out_specs=[VMEM] * 3,
        scratch_shapes=scratch,
        out_shape=[
            jax.ShapeDtypeStruct((4, 4, 128, 128), jnp.float32),
            jax.ShapeDtypeStruct((4, 4, 128, 128), jnp.float32),
            jax.ShapeDtypeStruct((4, 8, 2, 2, 128, 128), jnp.float32),
        ],
        cost_estimate=pl.CostEstimate(flops=0, bytes_accessed=0, transcendentals=0),
        compiler_params=pltpu.CompilerParams(vmem_limit_bytes=FAR_MIB * MIB),
        name="last",
    )(factors, inverse, partial, *far_panels[3:])

    traced = pl.pallas_call(
        trace_kernel,
        in_specs=[VMEM] * 9,
        out_specs=VMEM,
        out_shape=jax.ShapeDtypeStruct((4, 128, 256), jnp.float32),
        cost_estimate=pl.CostEstimate(flops=0, bytes_accessed=0, transcendentals=0),
        compiler_params=pltpu.CompilerParams(vmem_limit_bytes=TRACE_MIB * MIB),
        name="trace",
    )(factors, parts, diag_inverse, own_t, from_left, from_right, *theirs)
    from_left2, from_right2 = gate((from_left2, from_right2), traced)
    mine = [own_t, from_left, from_right, from_left2, from_right2]
    theirs = theirs + [other_core(piece) for piece in mine[3:]]

    def small(body, name, shape, *operands):
        return pl.pallas_call(
            body,
            in_specs=([VMEM] * 2 + [ANY]) if len(operands) == 3 else [VMEM] * len(operands),
            out_specs=[VMEM] * 4,
            out_shape=[jax.ShapeDtypeStruct(shape, jnp.float32)] * 4,
            cost_estimate=pl.CostEstimate(flops=0, bytes_accessed=MIB, transcendentals=0),
            compiler_params=pltpu.CompilerParams(vmem_limit_bytes=8 * MIB),
            name=name,
        )(*operands)

    (send,) = gate((send,), *theirs[3:])
    density = small(pair_kernel, "pair", (4, 128, 128), keep, other_core(send))
    t_keep, t_send = pl.pallas_call(
        rest_kernel,
        in_specs=[VMEM] * 6,
        out_specs=[VMEM] * 2,
        scratch_shapes=[pltpu.VMEM((4, 128, 256), jnp.float32)],
        out_shape=[jax.ShapeDtypeStruct((4, 64, 128), jnp.float32)] * 2,
        cost_estimate=pl.CostEstimate(flops=4 * 128 * 256 * 1024, bytes_accessed=MIB, transcendentals=0),
        compiler_params=pltpu.CompilerParams(vmem_limit_bytes=TRACE_MIB * MIB),
        name="rest",
    )(parts, traced, *mine[3:], *theirs[3:])
    diag = small(pair_kernel, "cores", (64, 128), t_keep, other_core(t_send), density[0])
    density = [density[0]] + [y_partner(density[bits], bits) for bits in (1, 2, 3)]
    diag = sum([x_partner(diag[bits], bits) for bits in (1, 2, 3)], diag[0])
    halves = [diag, z_partner(diag, 6)]
    diag = small(add_kernel, "nodes", (32, 128), *halves)
    diag = [diag[0]] + [y_partner(diag[bits], bits) for bits in (1, 2, 3)]
    joint = small(join_kernel, "join", (160, 128), *density, *diag)
    joint = [joint[0]] + [z_partner(joint[bits], bits) for bits in (1, 2, 3)]
    density, diag = pl.pallas_call(
        finish_kernel,
        in_specs=[SMEM] + [VMEM] * 4,
        out_specs=[VMEM] * 2,
        scratch_shapes=[pltpu.VMEM((128, 32), jnp.float32)],
        out_shape=[
            jax.ShapeDtypeStruct((128, 128), jnp.float32),
            jax.ShapeDtypeStruct((8, 32), jnp.float32),
        ],
        cost_estimate=pl.CostEstimate(flops=0, bytes_accessed=MIB, transcendentals=0),
        compiler_params=pltpu.CompilerParams(vmem_limit_bytes=8 * MIB),
        name="finish",
    )(ancestor_mask, *joint)
    return density, diag


def solution(mesh):
    placed = (
        P("pole", "blk", None),
        P("pole", "blk", None),
        P("blk", None),
        P("pole", "blk", None),
        P(),
        P(),
    )
    return jax.shard_map(
        per_device,
        mesh=mesh,
        in_specs=placed,
        out_specs=(P("blk", "pole"), P("blk", "pole")),
        check_vma=False,
    )
```

```python
import jax
import jax.numpy as jnp
from jax import lax
from jax.experimental import pallas as pl
from jax.experimental.pallas import tpu as pltpu
from jax.sharding import PartitionSpec as P

X, Z, C, Y = 4, 8, 2, 4
ROWS = 512
VMEM = pl.BlockSpec(memory_space=pltpu.VMEM)
SMEM = pl.BlockSpec(memory_space=pltpu.SMEM)
ANY = pl.BlockSpec(memory_space=pl.ANY)
HBM = pl.BlockSpec(memory_space=pltpu.HBM)
MIB = 2**20
NEAR_MIB, FAR_MIB, TRACE_MIB = 8, 10, 8


def place(x, z, core):
    return (x % X) * Z * C + (z % Z) * C + core


PLACES = [(x, z, core) for x in range(X) for z in range(Z) for core in range(C)]


def along_x(value, by):
    return lax.ppermute(value, "blk", [(place(*at), place(at[0] + by, at[1], at[2])) for at in PLACES])


def along_z(value, by):
    return lax.ppermute(value, "blk", [(place(*at), place(at[0], at[1] + by, at[2])) for at in PLACES])


def x_partner(value, bits):
    return lax.ppermute(value, "blk", [(place(*at), place(at[0] ^ bits, at[1], at[2])) for at in PLACES])


def z_partner(value, bits):
    return lax.ppermute(value, "blk", [(place(*at), place(at[0], at[1] ^ bits, at[2])) for at in PLACES])


def other_core(value):
    return lax.ppermute(value, "blk", [(place(*at), place(at[0], at[1], 1 - at[2])) for at in PLACES])


def y_partner(value, bits):
    return lax.ppermute(value, "pole", [(y, y ^ bits) for y in range(Y)])


def coordinates():
    rank = lax.axis_index("blk")
    return lax.axis_index("pole"), rank >> 4, (rank >> 1) & 7, rank & 1


def columns_of(x, side):
    return [(((x + by) & 3) * 2 + side) * 256 for by in (0, 3, 1, 2)]


def mask_kernel(mask, panel, own):
    for k in range(4):
        for t in range(2):
            part = slice(t * 512 + k * 128, t * 512 + k * 128 + 128)
            value = panel[:, :, part]
            own[:, :, part] = jnp.where(mask[0, k] != 0, value, jnp.zeros_like(value))


def factor_kernel(order, weights, token, factors):
    y, _, _, _ = coordinates()
    column = lax.broadcasted_iota(jnp.int32, (2, 8), 1)
    for p in range(2):
        chosen = jnp.where(column == order[y * 2 + p], weights[...], 0.0)
        factors[2 * p : 2 * p + 2, :] = jnp.broadcast_to(jnp.sum(chosen, axis=1, keepdims=True), (2, 512))


def build_form(form, panels):
    for step, panel_ref in enumerate(panels):
        top = step * 256
        form[top : top + 128, :] = panel_ref[...]
        form[top + 128 : top + 256, :512] = -panel_ref[:, 512:]
        form[top + 128 : top + 256, 512:] = panel_ref[:, :512]


def load_kernel(inverse, token, out, sems):
    copies = [
        pltpu.make_async_copy(
            inverse.at[p, pl.ds(half * 512, 512)], out.at[p, pl.ds(half * 512, 512)], sems.at[p, half]
        )
        for p in range(2)
        for half in range(2)
    ]
    for copy in copies:
        copy.start()
    for copy in copies:
        copy.wait()


def relay_kernel(right, left, token, relay_right, relay_left):
    relay_right[...] = right[0]
    relay_left[...] = left[1]


def multiply(inverse, panels, form, columns, use):
    for p in range(2):
        build_form(form, panels[p])

        @pl.loop(0, 1024 // ROWS)
        def _(tile):
            top = pl.multiple_of(tile * ROWS, ROWS)
            blocks = [inverse[p, pl.ds(top, ROWS), pl.ds(pl.multiple_of(at, 256), 256)] for at in columns]
            left = jnp.concatenate(blocks, axis=1) if len(blocks) > 1 else blocks[0]
            depth = 256 * len(columns)
            use(p, tile, jnp.dot(left, form[:depth, :], preferred_element_type=jnp.float32))


def first_kernel(inverse, own, right, left, across0, across1, out, form):
    across = (across0, across1)
    _, x, z, _ = coordinates()

    def use(p, tile, value):
        out[p, pl.ds(pl.multiple_of(tile * ROWS, ROWS), ROWS), :] = value

    panels = [[own.at[p], right.at[p], left.at[p], across[p]] for p in range(2)]
    multiply(inverse, panels, form, columns_of(x, z >> 2), use)


def middle_kernel(inverse, before, own, right, left, *rest):
    out, form = rest[-2:]
    _, x, z, _ = coordinates()

    def use(p, tile, value):
        rows = pl.ds(pl.multiple_of(tile * ROWS, ROWS), ROWS)
        out[p, rows, :] = before[p, rows, :] + value

    panels = [[own.at[p], right.at[p], left.at[p]] for p in range(2)]
    multiply(inverse, panels, form, columns_of(x, 1 - (z >> 2))[:3], use)


def last_kernel(factors, inverse, before, across0, across1, keep, send, parts, form):
    y, x, z, core = coordinates()
    zl = z & 3

    def use(p, tile, value):
        w_re, w_im = factors[2 * p : 2 * p + 1, :], factors[2 * p + 1 : 2 * p + 2, :]
        total = before[p, pl.ds(pl.multiple_of(tile * ROWS, ROWS), ROWS), :] + value
        real, imag = total[:, :512], total[:, 512:]
        q_re = w_re * real - w_im * imag
        q_im = -(w_re * imag + w_im * real)
        for k in range(4):
            part = slice(k * 128, k * 128 + 128)
            for c in range(ROWS // 128):
                for side, q in enumerate((q_re, q_im)):
                    parts[k, tile * (ROWS // 128) + c, p, side] = q[c * 128 : c * 128 + 128, part]
            for pair in range(ROWS // 256):
                near = (tile * (ROWS // 256) + pair) ^ zl
                even = q_re[pair * 256 : pair * 256 + 128, part]
                odd = q_re[pair * 256 + 128 : pair * 256 + 256, part]
                kept = jnp.where(core == 0, even, odd)
                sent = jnp.where(core == 0, odd, even)
                if p == 0:
                    keep[k ^ y, near] = -kept
                    send[k ^ y, near] = -sent
                else:
                    keep[k ^ y, near] = keep[k ^ y, near] - kept
                    send[k ^ y, near] = send[k ^ y, near] - sent

    multiply(inverse, [[across0], [across1]], form, columns_of(x, 1 - (z >> 2))[3:], use)


def flip_kernel(panel, token0, token1, token2, token3, out):
    for p in range(2):
        for part in range(8):
            out[p, part] = panel[p, :, part * 128 : part * 128 + 128].T


def hop_kernel(far, from_left, from_right, token, to_right, to_left):
    _, _, z, _ = coordinates()
    zl = z & 3
    for edge, got, out in ((3, from_left, to_right), (0, from_right, to_left)):
        @pl.when(zl == edge)
        def _():
            for p in range(2):
                for part in range(8):
                    out[p, part] = far[p, :, part * 128 : part * 128 + 128].T

        @pl.when(zl != edge)
        def _():
            out[...] = got[...]


def gate_kernel(*refs):
    pass


def pair_kernel(keep, got, *rest):
    outs = rest[-4:]
    for bits in range(4):
        outs[bits][...] = keep[bits] + got[bits]


def add_kernel(a, b, *outs):
    y, _, _, _ = coordinates()
    total = (a[...] + b[...]).T
    for target in range(4):
        for bits in range(4):
            @pl.when((y ^ bits) == target)
            def _():
                outs[bits][:, :64] = total[target * 32 : target * 32 + 32]
                outs[bits][:, 64:] = jnp.zeros((32, 64), jnp.float32)


def join_kernel(*refs):
    density, diag, outs = refs[:4], refs[4:8], refs[8:]
    small = (diag[0][...] + diag[1][...]) + (diag[2][...] + diag[3][...])
    for bits in range(4):
        outs[bits][:128] = (density[0][bits] + density[1][bits]) + (density[2][bits] + density[3][bits])
        outs[bits][128:] = small


def trace_kernel(factors, parts, diag, *rest):
    pieces, keep, send, total = rest[:10], rest[10], rest[11], rest[12]
    y, x, z, core = coordinates()
    zl = z & 3
    total[...] = jnp.zeros_like(total)
    rows_at = [
        zl,
        jnp.where(zl == 0, -1, zl - 1),
        jnp.where(zl == 3, -1, zl + 1),
        jnp.where(zl == 0, 3, jnp.where(zl == 1, -1, zl - 2)),
        jnp.where(zl == 3, 0, jnp.where(zl == 2, -1, zl + 2)),
    ]
    for index, piece in enumerate(pieces):
        row = rows_at[index % 5]
        c = row * 2 + (core if index < 5 else 1 - core)

        @pl.when(row >= 0)
        def _():
            for k in range(4):
                left = jnp.concatenate(
                    [piece[p, side * 4 + k] for p in range(2) for side in range(2)], axis=1
                )
                right = parts[k, c].reshape(512, 128)
                high = right.astype(jnp.bfloat16)
                low = (right - high.astype(jnp.float32)).astype(jnp.bfloat16)
                total[k] += jnp.dot(
                    left, jnp.concatenate([high, low], axis=1), preferred_element_type=jnp.float32
                )

    mine = jnp.zeros((8, 128), jnp.float32)
    for p in range(2):
        w_re, w_im = factors[2 * p : 2 * p + 1, :128], factors[2 * p + 1 : 2 * p + 2, :128]
        mine += w_re * diag[p, :, :128] - w_im * diag[p, :, 128:]
    row = pl.multiple_of((z * 2 + core) * 8, 8)
    total[x, pl.ds(row, 8), :128] = total[x, pl.ds(row, 8), :128] + mine
    for k in range(4):
        value = (total[k, :, :128] + total[k, :, 128:]).reshape(8, 2, 8, 128)
        keep[k ^ x] = jnp.where(core == 0, value[:, 0], value[:, 1]).reshape(64, 128)
        send[k ^ x] = jnp.where(core == 0, value[:, 1], value[:, 0]).reshape(64, 128)


def finish_kernel(mask, a, b, c, d, density, diag, flipped):
    y, _, z, _ = coordinates()
    total = (a[...] + b[...]) + (c[...] + d[...])
    density[...] = jnp.where(mask[0, y] != 0, total[:128], 0.0)
    flipped[...] = total[128:].T
    diag[...] = flipped[pl.ds(pl.multiple_of(z * 8, 8), 8), :]


def per_device(inverse_blocks, panel_blocks, ancestor_mask, diag_inverse, pole_weights, pole_order):
    y, xc, z, core = coordinates()
    zl = z & 3

    own = pl.pallas_call(
        mask_kernel,
        in_specs=[SMEM, VMEM],
        out_specs=VMEM,
        out_shape=jax.ShapeDtypeStruct((2, 128, 1024), jnp.bfloat16),
        cost_estimate=pl.CostEstimate(flops=0, bytes_accessed=MIB, transcendentals=0),
        compiler_params=pltpu.CompilerParams(vmem_limit_bytes=8 * MIB),
        name="mask",
    )(ancestor_mask, panel_blocks)
    factors = pl.pallas_call(
        factor_kernel,
        in_specs=[SMEM, VMEM, ANY],
        out_specs=VMEM,
        out_shape=jax.ShapeDtypeStruct((4, 512), jnp.float32),
        cost_estimate=pl.CostEstimate(flops=0, bytes_accessed=8192, transcendentals=0),
        compiler_params=pltpu.CompilerParams(vmem_limit_bytes=8 * MIB),
        name="factors",
    )(pole_order, pole_weights.T, own)
    def gate(values, *tokens, weight=0):
        return pl.pallas_call(
            gate_kernel,
            in_specs=[ANY] * (len(values) + len(tokens)),
            out_specs=[ANY] * len(values),
            out_shape=[jax.ShapeDtypeStruct(value.shape, value.dtype) for value in values],
            input_output_aliases={at: at for at in range(len(values))},
            cost_estimate=pl.CostEstimate(flops=0, bytes_accessed=weight, transcendentals=0),
            compiler_params=pltpu.CompilerParams(vmem_limit_bytes=MIB),
            name="gate",
        )(*values, *tokens)

    (far,) = gate((z_partner(own, 4),), weight=0)
    right, left = along_x(own, 1), along_x(own, -1)
    def relay(right, left, token):
        halves = pl.pallas_call(
            relay_kernel,
            in_specs=[VMEM] * 2 + [ANY],
            out_specs=[VMEM] * 2,
            out_shape=[jax.ShapeDtypeStruct((128, 1024), jnp.bfloat16)] * 2,
            cost_estimate=pl.CostEstimate(flops=0, bytes_accessed=MIB, transcendentals=0),
            compiler_params=pltpu.CompilerParams(vmem_limit_bytes=8 * MIB),
            name="relay",
        )(right, left, token)
        return halves

    halves = relay(right, left, own)
    near_panels = [own, right, left, along_x(halves[0], 1), along_x(halves[1], -1)]
    far_right, far_left = along_x(far, 1), along_x(far, -1)

    scratch = [pltpu.VMEM((1024, 1024), jnp.bfloat16)]
    inverse = pl.pallas_call(
        load_kernel,
        in_specs=[HBM, ANY],
        out_specs=VMEM,
        scratch_shapes=[pltpu.SemaphoreType.DMA((2, 2))],
        out_shape=jax.ShapeDtypeStruct((2, 1024, 2048), jnp.bfloat16),
        cost_estimate=pl.CostEstimate(flops=0, bytes_accessed=16 * MIB, transcendentals=0),
        compiler_params=pltpu.CompilerParams(vmem_limit_bytes=10 * MIB),
        name="load",
    )(inverse_blocks, factors)
    def flip(panel, *tokens):
        return pl.pallas_call(
            flip_kernel,
            in_specs=[VMEM] + [ANY] * 4,
            out_specs=VMEM,
            out_shape=jax.ShapeDtypeStruct((2, 8, 128, 128), jnp.bfloat16),
            cost_estimate=pl.CostEstimate(flops=0, bytes_accessed=MIB, transcendentals=0),
            compiler_params=pltpu.CompilerParams(vmem_limit_bytes=8 * MIB),
            name="flip",
        )(panel, *tokens)

    own_t = flip(own, far, *near_panels[3:], inverse)
    partial = pl.pallas_call(
        first_kernel,
        in_specs=[VMEM] * 6,
        out_specs=VMEM,
        scratch_shapes=scratch,
        out_shape=jax.ShapeDtypeStruct((2, 1024, 1024), jnp.float32),
        cost_estimate=pl.CostEstimate(flops=2 * 2 * 1024**3, bytes_accessed=4 * MIB, transcendentals=0),
        compiler_params=pltpu.CompilerParams(vmem_limit_bytes=NEAR_MIB * MIB),
        name="near",
    )(inverse, *near_panels)

    from_left, from_right = along_z(own_t, 1), along_z(own_t, -1)
    from_left, from_right = gate((from_left, from_right), partial)
    to_right, to_left = pl.pallas_call(
        hop_kernel,
        in_specs=[VMEM] * 3 + [ANY],
        out_specs=[VMEM] * 2,
        out_shape=[jax.ShapeDtypeStruct((2, 8, 128, 128), jnp.bfloat16)] * 2,
        cost_estimate=pl.CostEstimate(flops=0, bytes_accessed=2 * MIB, transcendentals=0),
        compiler_params=pltpu.CompilerParams(vmem_limit_bytes=8 * MIB),
        name="hop",
    )(far, from_left, from_right, partial)
    from_left2, from_right2 = along_z(to_right, 1), along_z(to_left, -1)
    halves = relay(far_right, far_left, to_right)
    far_panels = [far, far_right, far_left, along_x(halves[0], 1), along_x(halves[1], -1)]
    theirs = [other_core(piece) for piece in (own_t, from_left, from_right)]

    partial = pl.pallas_call(
        middle_kernel,
        in_specs=[VMEM] * 5 + [ANY] * 3,
        out_specs=VMEM,
        scratch_shapes=scratch,
        out_shape=jax.ShapeDtypeStruct((2, 1024, 1024), jnp.float32),
        input_output_aliases={1: 0},
        cost_estimate=pl.CostEstimate(flops=3 * 1024**3, bytes_accessed=4 * MIB, transcendentals=0),
        compiler_params=pltpu.CompilerParams(vmem_limit_bytes=NEAR_MIB * MIB),
        name="middle",
    )(inverse, partial, *far_panels[:3], *theirs)

    keep, send, parts = pl.pallas_call(
        last_kernel,
        in_specs=[VMEM] * 5,
        out_specs=[VMEM] * 3,
        scratch_shapes=scratch,
        out_shape=[
            jax.ShapeDtypeStruct((4, 4, 128, 128), jnp.float32),
            jax.ShapeDtypeStruct((4, 4, 128, 128), jnp.float32),
            jax.ShapeDtypeStruct((4, 8, 2, 2, 128, 128), jnp.float32),
        ],
        cost_estimate=pl.CostEstimate(flops=0, bytes_accessed=0, transcendentals=0),
        compiler_params=pltpu.CompilerParams(vmem_limit_bytes=FAR_MIB * MIB),
        name="last",
    )(factors, inverse, partial, *far_panels[3:])

    from_left2, from_right2 = gate((from_left2, from_right2), keep)
    mine = [own_t, from_left, from_right, from_left2, from_right2]
    theirs = theirs + [other_core(piece) for piece in mine[3:]]
    (send,) = gate((send,), *theirs[3:])

    def small(body, name, shape, *operands):
        return pl.pallas_call(
            body,
            in_specs=([VMEM] * 2 + [ANY]) if len(operands) == 3 else [VMEM] * len(operands),
            out_specs=[VMEM] * 4,
            out_shape=[jax.ShapeDtypeStruct(shape, jnp.float32)] * 4,
            cost_estimate=pl.CostEstimate(flops=0, bytes_accessed=MIB, transcendentals=0),
            compiler_params=pltpu.CompilerParams(vmem_limit_bytes=8 * MIB),
            name=name,
        )(*operands)

    density = small(pair_kernel, "pair", (4, 128, 128), keep, other_core(send))
    t_keep, t_send = pl.pallas_call(
        trace_kernel,
        in_specs=[VMEM] * 13,
        out_specs=[VMEM] * 2,
        scratch_shapes=[pltpu.VMEM((4, 128, 256), jnp.float32)],
        out_shape=[jax.ShapeDtypeStruct((4, 64, 128), jnp.float32)] * 2,
        cost_estimate=pl.CostEstimate(flops=2 * 4 * 128 * 256 * 4096, bytes_accessed=4 * MIB, transcendentals=0),
        compiler_params=pltpu.CompilerParams(vmem_limit_bytes=TRACE_MIB * MIB),
        name="trace",
    )(factors, parts, diag_inverse, *mine, *theirs)
    diag = small(pair_kernel, "cores", (64, 128), t_keep, other_core(t_send))
    density = [density[0]] + [y_partner(density[bits], bits) for bits in (1, 2, 3)]
    diag = sum([x_partner(diag[bits], bits) for bits in (1, 2, 3)], diag[0])
    halves = [diag, z_partner(diag, 6)]
    diag = small(add_kernel, "nodes", (32, 128), *halves)
    diag = [diag[0]] + [y_partner(diag[bits], bits) for bits in (1, 2, 3)]
    joint = small(join_kernel, "join", (160, 128), *density, *diag)
    joint = [joint[0]] + [z_partner(joint[bits], bits) for bits in (1, 2, 3)]
    density, diag = pl.pallas_call(
        finish_kernel,
        in_specs=[SMEM] + [VMEM] * 4,
        out_specs=[VMEM] * 2,
        scratch_shapes=[pltpu.VMEM((128, 32), jnp.float32)],
        out_shape=[
            jax.ShapeDtypeStruct((128, 128), jnp.float32),
            jax.ShapeDtypeStruct((8, 32), jnp.float32),
        ],
        cost_estimate=pl.CostEstimate(flops=0, bytes_accessed=MIB, transcendentals=0),
        compiler_params=pltpu.CompilerParams(vmem_limit_bytes=8 * MIB),
        name="finish",
    )(ancestor_mask, *joint)
    return density, diag


def solution(mesh):
    placed = (
        P("pole", "blk", None),
        P("pole", "blk", None),
        P("blk", None),
        P("pole", "blk", None),
        P(),
        P(),
    )
    return jax.shard_map(
        per_device,
        mesh=mesh,
        in_specs=placed,
        out_specs=(P("blk", "pole"), P("blk", "pole")),
        check_vma=False,
    )
```
